32 devices in a mesh: grp: 2 (over y), freq: 4 (over z), tri: 2 (over x), sta: 2 (over core).
Axes of the slice: x: 2, y: 2, z: 4, core: 2. Of those that a mesh axis runs over, the one named last changes fastest.
Arguments:
- slip: float32 [8, 8192], P(None, ('grp', 'freq', 'tri')), parts along dimension 1, may hold values from 0 to 1
- green: float32 [32, 8, 64, 128], P('freq'), may hold values from -0.09375 to 0.09375
- pattern: int32 [64, 64], P('sta'), may hold values from -1 to 7
- observed: float32 [2, 64, 4096], P(None, ('grp', 'freq'), 'sta'), parts along dimension 1, may hold values from -6 to 6
- adjacency: int32 [3, 2048], P(None, ('freq', 'tri')), may hold values from 0 to 2047, as said below
- smooth_weight: float32 [2], P('grp'), parts along dimension 0, may hold values from 2 to 8
Outputs:
- new_slip: float32 [8, 8192], P(None, ('grp', 'freq', 'tri')), parts along dimension 1
- residual: float32 [2, 64, 4096], P(None, ('grp', 'freq'), 'sta'), parts along dimension 1
The draws below stay inside these ranges and needn't reach their ends.
There are 2 independent parts, one for each index of `grp`. The reference program is written for one: setup_inputs(seed, part) draws one part's arguments, and reference() takes and returns one part's arrays. A program takes and returns all parts, laid end to end along the dimension named above; an argument that names none is the same for every part. Nothing has to cross between parts.
Inputs may be any that keep to these rules, and one draw needn't show every extreme that they name: adjacency[j, t] differs from t by 1 to 256, and adjacency[0, t] differs from t by exactly 256. `pattern`: -1 marks an absent block.
All inputs are finite; a program needn't handle non-finite values.
Results may differ from the reference program's by a relative error of at most 0.000058.
Values sent between devices are 32-bit elements; how exact they have to be, the bound alone decides.
No kernel may reach another device: no remote copies, remote signals or barrier semaphores. Data moves between devices by JAX's collectives and lax.ppermute only.
A program may use at most 64 MiB of HBM per device.

```python
import math
import jax
import jax.numpy as jnp
from jax import lax

BLK = 64
NW = 8
NDIST = 8
TRI_DEV = 256
NF = 32
NT = 2048
NCOL = 4096
NS = 4096
SB = 64
CB = 64


def draw_adjacency(key, part):
    positions = jnp.arange(NT, dtype=jnp.int32)
    reach = jax.random.randint(jax.random.fold_in(key, 11), (2, NT), 1, TRI_DEV + 1)
    reach = jnp.concatenate([jnp.full((1, NT), TRI_DEV, dtype=jnp.int32), reach], axis=0)
    direction = jax.random.randint(jax.random.fold_in(key, 12), (3, NT), 0, 2) * 2 - 1
    offset = reach * direction
    target = positions[None, :] + offset
    target = jnp.where((target < 0) | (target >= NT), positions[None, :] - offset, target)
    return target.astype(jnp.int32)


def touch_ends(array, stream_key, smallest, top_value):
    shape = array.shape
    place = [jax.random.randint(jax.random.fold_in(stream_key, axis), (), 0, shape[axis]) for axis in range(len(shape))]
    array = array.at[tuple(place)].set(smallest)
    longest = shape.index(max(shape))
    place[longest] = (place[longest] + 1) % shape[longest]
    return array.at[tuple(place)].set(top_value)


def steps_of(stream_key, shape, shards, smallest, high):
    factor_of = 1.0
    for dim, parts in shards:
        steps = jax.random.uniform(jax.random.fold_in(jax.random.fold_in(stream_key, 6), dim), (parts,), jnp.float32, smallest / len(shards), high / len(shards))
        factor_of = factor_of * jnp.repeat(jnp.exp(steps), shape[dim] // parts).reshape((-1,) + (1,) * (len(shape) - 1 - dim))
    return factor_of


def noise(rng, shape, spread, limit, pieces=(), kind=jnp.bfloat16):
    gain = steps_of(rng, shape, pieces, -0.22, 0.18) if pieces else 1.0
    values = jax.random.normal(rng, shape, jnp.float32) * spread * gain
    return jnp.minimum(jnp.maximum(values, -limit), limit).astype(kind)


def setup_inputs(seed: int = 0, part: int = 0) -> dict:
    streams_of = jax.random.split(jax.random.key(seed), 7)
    part_splits = jax.random.split(jax.random.fold_in(streams_of[6], part), 7)
    slip = jnp.clip(1.0 * jax.random.uniform(part_splits[0], (NW, NCOL), jnp.float32) ** steps_of(part_splits[0], (NW, NCOL), ((1, 8),), -0.2, 0.2), 0.0, 1.0)
    green = noise(streams_of[1], (NF, NDIST, BLK, 2 * BLK), NCOL ** -0.5, 0.09375, ((0, 4),), jnp.float32)
    pattern = touch_ends(jax.random.randint(streams_of[2], (SB, CB), -1, NDIST), jax.random.fold_in(streams_of[2], 1), -1, NDIST - 1).astype(jnp.int32)
    observed = noise(part_splits[3], (2, NF, NS), 1.0, 6.0, ((1, 4), (2, 2)), jnp.float32)
    adjacency = draw_adjacency(jax.random.fold_in(streams_of[6], 71), part)
    smooth_weight = jnp.clip(jnp.exp(jax.random.uniform(part_splits[5], (1,), jnp.float32, math.log(2.0), math.log(8.0))), 2.0, 8.0)
    return dict(slip=slip, green=green, pattern=pattern, observed=observed, adjacency=adjacency, smooth_weight=smooth_weight)


PRECISE = lax.Precision.HIGHEST


def phase_tables(first_freq, freq_count, freq_total, windows):
    frequency = jnp.arange(freq_count, dtype=jnp.float32) + first_freq + 1.0
    window = jnp.arange(windows, dtype=jnp.float32) + 0.5
    phases = (4.0 * math.pi / freq_total) * frequency[:, None] * window[None, :]
    return jnp.cos(phases), -jnp.sin(phases)


def onehot_table(pattern, classes):
    return (pattern[:, None, :] == jnp.arange(classes, dtype=jnp.int32)[None, :, None]).astype(jnp.float32)


def apply_green(spectra, green, onehot, block):
    freqs = spectra.shape[1]
    columns = spectra.reshape(2, freqs, -1, block)
    summed = jnp.einsum('skc,rfcx->rfskx', onehot, columns, precision=PRECISE)
    green_real = green[:, :, :, :block]
    green_imag = green[:, :, :, block:]

    def product(left, right):
        return jnp.einsum('fkyx,fskx->fsy', left, right, precision=PRECISE)

    real_part = product(green_real, summed[0]) - product(green_imag, summed[1])
    imag_part = product(green_real, summed[1]) + product(green_imag, summed[0])
    return jnp.stack([real_part, imag_part]).reshape(2, freqs, -1)


def adjoint_green(misfit, green, onehot, block):
    freqs = misfit.shape[1]
    blocks = misfit.reshape(2, freqs, -1, block)
    green_real = green[:, :, :, :block]
    green_imag = green[:, :, :, block:]

    def product(left, right):
        return jnp.einsum('fkyx,fsy->fskx', left, right, precision=PRECISE)

    real_part = product(green_real, blocks[0]) + product(green_imag, blocks[1])
    imag_part = product(green_real, blocks[1]) - product(green_imag, blocks[0])
    result = jnp.einsum('skc,rfskx->rfcx', onehot, jnp.stack([real_part, imag_part]), precision=PRECISE)
    return result.reshape(2, freqs, -1)


def reference(slip, green, pattern, observed, adjacency, smooth_weight):
    smoothing = smooth_weight[0]
    cos_table, sin_table = phase_tables(0, NF, NF, NW)
    onehot = onehot_table(pattern, NDIST)

    def to_spectra(field):
        return jnp.stack([jnp.dot(cos_table, field, precision=PRECISE), jnp.dot(sin_table, field, precision=PRECISE)])

    predicted = apply_green(to_spectra(slip), green, onehot, BLK)
    residual = predicted - observed
    adjoint_part = adjoint_green(residual, green, onehot, BLK)
    data_grad = jnp.dot(cos_table.T, adjoint_part[0], precision=PRECISE) + jnp.dot(sin_table.T, adjoint_part[1], precision=PRECISE)
    slip_grid = slip.reshape(NW, NT, 2)
    neighbour_mean = (slip_grid[:, adjacency[0]] + slip_grid[:, adjacency[1]] + slip_grid[:, adjacency[2]]) / 3.0
    gradient = data_grad + smoothing * (slip - neighbour_mean.reshape(NW, NCOL))
    image_data = apply_green(to_spectra(gradient), green, onehot, BLK)
    numerator = jnp.sum(gradient * gradient)
    denominator = jnp.sum(image_data * image_data) + smoothing * numerator
    step_length = numerator / denominator
    new_slip = jnp.maximum(slip - step_length * gradient, 0.0)
    return new_slip, residual
```

```python
import math

import jax
import jax.numpy as jnp
import numpy as np
from jax import lax
from jax.experimental import pallas as pl
from jax.experimental.pallas import tpu as pltpu
from jax.sharding import PartitionSpec as P

F32 = jnp.float32
BF16 = jnp.bfloat16
LANES = 128
CHUNK = 64
SHARD_ROWS = 16


def phase_table(freq_total, windows, block):
    frequency = np.arange(freq_total, dtype=np.float32) + np.float32(1.0)
    window = np.arange(windows, dtype=np.float32) + np.float32(0.5)
    phases = np.float32(4.0 * math.pi / freq_total) * frequency[:, None] * window[None, :]
    phases = phases.astype(np.float64)
    both = np.stack([np.cos(phases), -np.sin(phases)], axis=-1).astype(np.float32)
    return np.repeat(both, block, axis=-1)


def split(value):
    high = value.astype(BF16)
    return high, (value - high.astype(F32)).astype(BF16)


def low_lanes(shape, block):
    return lax.broadcasted_iota(jnp.int32, shape, len(shape) - 1) < block


def spread_columns(read, parts, spread):
    def one(p, carry):
        value = read(p)
        for j in range(value.shape[1] // LANES):
            piece = value[:, j * LANES : (j + 1) * LANES]
            turned = pltpu.roll(piece, LANES // 2, 1)
            low = low_lanes(piece.shape, LANES // 2)
            row = (p * (value.shape[1] // LANES) + j) * 16
            row = row if isinstance(row, int) else pl.multiple_of(row, 16)
            spread[pl.ds(row, 8), :] = jnp.where(low, piece, turned)
            spread[pl.ds(row + 8, 8), :] = jnp.where(low, turned, piece)
        return carry

    if parts <= 8:
        for p in range(parts):
            one(p, 0)
    else:
        lax.fori_loop(0, parts, one, 0)


def onehot_of(pattern, classes):
    doubled = jnp.concatenate([pattern, pattern], axis=1)
    return jnp.concatenate(
        [(doubled == k).astype(F32).astype(BF16) for k in range(classes)], axis=0
    )


def over_chunks(count, step):
    if count == 1:
        step(0)
    else:
        lax.fori_loop(0, count, lambda n, carry: (step(n), carry)[1], 0)


def pattern_sums(spread, table, first, pattern_ref, summed, freqs, classes):
    windows = table.shape[1]

    def step(n):
        base = n * CHUNK * windows
        fields = [spread[pl.ds(base + w, CHUNK, stride=windows), :] for w in range(windows)]
        spectra = []
        for f in range(freqs):
            row = table[first + f]
            total = row[0:1] * fields[0]
            for w in range(1, windows):
                total = total + row[w : w + 1] * fields[w]
            spectra.append(jnp.concatenate(split(total), axis=0))
        product = jnp.dot(
            onehot_of(pattern_ref[n], classes),
            jnp.concatenate(spectra, axis=1),
            preferred_element_type=F32,
        )
        if isinstance(n, int):
            summed[...] = product
        else:
            summed[...] += product

    chunks = pattern_ref.shape[0]
    if chunks > 1:
        summed[...] = jnp.zeros_like(summed)
    over_chunks(chunks, step)


def green_rows(green_ref, f):
    pieces = [
        jnp.concatenate(split(green_ref[f, k]), axis=0) for k in range(green_ref.shape[1])
    ]
    return jnp.concatenate(pieces, axis=1)


def predict_one(summed, green, f, classes, stations, block):
    value = summed[:, f * LANES : (f + 1) * LANES]
    sign = jnp.where(low_lanes(value.shape, block), 1.0, -1.0)
    real = value * sign
    imag = pltpu.roll(value, block, 1)
    rows = []
    for half in zip(split(real), split(imag)):
        for part in half:
            rows.append(
                jnp.concatenate(
                    [part[k * stations : (k + 1) * stations] for k in range(classes)], axis=1
                )
            )
    left = jnp.concatenate(rows, axis=0)
    out = lax.dot_general(left, green, (((1,), (1,)), ((), ())), preferred_element_type=F32)
    high = out[: 2 * stations]
    low = out[2 * stations :]
    cross = jnp.where(low_lanes(low.shape, block), low, 0.0)
    total = high + cross
    return total + pltpu.roll(total, block, 1)


def forward_kernel(
    windows,
    place,
    shards,
    green_ref,
    pattern_ref,
    observed,
    table,
    residual_out,
    partial_out,
    spread,
    summed,
    apart,
    fields,
):
    freqs, classes, block, _ = green_ref.shape
    stations = pattern_ref.shape[1]
    parts = shards.shape[0]
    first = place[0] * freqs
    half = place[2]
    low8 = low_lanes((8, LANES), block)
    for r in range(2):
        for j in range(stations // 2):
            piece = observed[r, :, j * LANES : (j + 1) * LANES]
            apart[r, 2 * j * freqs : (2 * j + 1) * freqs, :] = piece
            apart[r, (2 * j + 1) * freqs : (2 * j + 2) * freqs, :] = pltpu.roll(piece, block, 1)
    spread_columns(lambda p: shards[p, :windows, :], parts, spread)
    pattern_sums(spread, table, first, pattern_ref, summed, freqs, classes)
    for f in range(freqs):
        green = green_rows(green_ref, f)
        predicted = predict_one(summed, green, f, classes, stations, block)
        low = low_lanes(predicted.shape, block)
        seen = jnp.concatenate(
            [apart[r, pl.ds(f, stations, stride=freqs), :] for r in range(2)], axis=0
        )
        misfit = predicted - seen
        for r in range(2):
            apart[r, pl.ds(f, stations, stride=freqs), :] = misfit[r * stations : (r + 1) * stations]
        misfit = jnp.where(low, misfit, pltpu.roll(misfit, block, 1))
        high, rest = split(misfit)
        left = jnp.concatenate([high, rest[:, :block]], axis=1)
        right = jnp.concatenate([green, green[:block]], axis=0)
        out = jnp.dot(left, right, preferred_element_type=F32)
        sign = jnp.where(low_lanes((stations, LANES), block), 1.0, -1.0)
        for k in range(classes):
            real = out[:stations, k * LANES : (k + 1) * LANES]
            imag = out[stations:, k * LANES : (k + 1) * LANES]
            summed[k * stations : (k + 1) * stations, f * LANES : (f + 1) * LANES] = (
                real * sign + pltpu.roll(imag, block, 1)
            )
    for r in range(2):
        for j in range(stations // 2):
            even = apart[r, 2 * j * freqs : (2 * j + 1) * freqs, :]
            odd = apart[r, (2 * j + 1) * freqs : (2 * j + 2) * freqs, :]
            residual_out[r, :, j * LANES : (j + 1) * LANES] = jnp.where(
                low8, even, pltpu.roll(odd, block, 1)
            )

    right = jnp.concatenate(split(summed[...]), axis=0)
    per_part = shards.shape[2] // block
    chunk_parts = CHUNK // per_part

    def step(n):
        onehot = onehot_of(pattern_ref[n], classes)[:, :block].astype(F32).T.astype(BF16)
        left = jnp.concatenate([onehot, onehot], axis=1)
        adjoint = jnp.dot(left, right, preferred_element_type=F32)
        for w in range(windows):
            total = table[first, w : w + 1, :] * adjoint[:, :LANES]
            for f in range(1, freqs):
                total = total + table[first + f, w : w + 1, :] * adjoint[:, f * LANES : (f + 1) * LANES]
            fields[pl.ds(w, CHUNK, stride=windows), :] = total + pltpu.roll(total, block, 1)
        for q in range(chunk_parts):
            p = n * chunk_parts + q
            side = lax.rem(p // (parts // 2) + half, 2)
            slot = lax.rem(jnp.asarray(p, jnp.int32), parts // 2)
            for j in range(per_part // 2):
                row = (q * per_part + 2 * j) * windows
                partial_out[side, slot, :, j * LANES : (j + 1) * LANES] = jnp.where(
                    low8, fields[row : row + windows, :], fields[row + windows : row + 2 * windows, :]
                )

    over_chunks(pattern_ref.shape[0], step)


def smooth_kernel(windows, place, weight, shards, out):
    parts, _, width = shards.shape
    count = out.shape[0]
    pieces = width // LANES
    lane = lax.broadcasted_iota(jnp.int32, (windows, LANES), 1)

    def pick(source, index):
        return jnp.take_along_axis(source, index, axis=1, mode="promise_in_bounds")

    def one(slot, carry):
        p = place[2] * count + slot
        around = [jnp.maximum(p - 1, 0), p, jnp.minimum(p + 1, parts - 1)]
        source = [
            shards[a, :windows, j * LANES : (j + 1) * LANES] for a in around for j in range(pieces)
        ]
        for q in range(pieces):
            total = None
            for j in range(3):
                row = shards[p, windows + j : windows + j + 1, (q // 2) * LANES : (q // 2 + 1) * LANES]
                row = jnp.broadcast_to(row, (windows, LANES))
                target = pick(row, (q % 2) * (LANES // 2) + lane // 2).astype(jnp.int32)
                column = 2 * target + lane % 2 - (p - 1) * width
                inside = jnp.bitwise_and(column, LANES - 1)
                which = jnp.right_shift(column, 7)
                value = jnp.zeros((windows, LANES), F32)
                for v in range(q, q + 2 * pieces + 1):
                    value = jnp.where(which == v, pick(source[v], inside), value)
                total = value if total is None else total + value
            own = source[pieces + q]
            out[slot, :, q * LANES : (q + 1) * LANES] = weight[0] * (own - total / 3.0)
        return carry

    lax.fori_loop(0, count, one, 0)


def image_kernel(
    place, mine, other, green_ref, pattern_ref, table, own_out, sums_out, spread, summed
):
    freqs, classes, block, _ = green_ref.shape
    stations = pattern_ref.shape[1]
    count, windows, width = mine.shape
    first = place[0] * freqs
    half = place[2]

    def read(p):
        slot = p % count if isinstance(p, int) else lax.rem(p, count)
        return jnp.where(p // count == half, mine[slot], other[slot])

    spread_columns(read, 2 * count, spread)
    pattern_sums(spread, table, first, pattern_ref, summed, freqs, classes)
    me = place[1]
    slot = lax.rem(me, count)
    own_out[...] = jnp.where(me // count == half, mine[slot], other[slot])

    def squares(p, total):
        value = read(p)
        value = value * value
        for j in range(width // LANES):
            total = total + value[:, j * LANES : (j + 1) * LANES]
        return total

    numerator = lax.fori_loop(0, 2 * count, squares, jnp.zeros((windows, LANES), F32), unroll=count <= 4)
    image = jnp.zeros((8, LANES), F32)
    for f in range(freqs):
        predicted = predict_one(summed, green_rows(green_ref, f), f, classes, stations, block)
        predicted = predicted * predicted
        for j in range(predicted.shape[0] // 8):
            image = image + predicted[8 * j : 8 * j + 8]
    image = jnp.where(low_lanes(image.shape, block), image, 0.0)
    sums_out[0] = jnp.broadcast_to(jnp.sum(image), (8, LANES))
    sums_out[1] = jnp.broadcast_to(jnp.sum(numerator), (8, LANES))


def update_kernel(count, weight, *refs):
    sums, slip, own, out = refs[0], refs[1 + count], refs[2 + count], refs[3 + count]
    image = sums[0]
    for r in refs[1 : 1 + count]:
        image = image + r[...]
    numerator = sums[1]
    step = numerator / (image + weight[0] * numerator)
    step = jnp.concatenate([step] * (slip.shape[1] // LANES), axis=1)
    out[...] = jnp.maximum(slip[...] - step * own[...], 0.0)


SMEM = pl.BlockSpec(memory_space=pltpu.SMEM)
VMEM = pl.BlockSpec(memory_space=pltpu.VMEM)


def local(slip, green, pattern, observed, adjacency, smooth_weight, *, table):
    n_freq, n_tri, n_sta = (lax.axis_size(a) for a in ("freq", "tri", "sta"))
    parts = n_freq * n_tri
    count = parts // n_sta
    freqs, classes, block, _ = green.shape
    windows, columns = slip.shape
    stations, blocks = pattern.shape
    index = [lax.axis_index(a) for a in (("freq",), ("freq", "tri"), ("sta",))]
    place = jnp.stack(index).astype(jnp.int32)
    pattern = pattern.reshape(stations, blocks // CHUNK, CHUNK).transpose(1, 0, 2)
    limit = pltpu.CompilerParams(vmem_limit_bytes=48 * 2**20)

    triangles = adjacency.shape[1]
    packed = jnp.concatenate(
        [
            slip,
            jnp.pad(
                adjacency.astype(F32),
                ((0, SHARD_ROWS - windows - adjacency.shape[0]), (0, columns - triangles)),
            ),
        ],
        axis=0,
    )
    shards = lax.all_to_all(
        jnp.broadcast_to(packed[None], (parts,) + packed.shape), ("freq", "tri"), 0, 0, tiled=True
    )

    flops = 2 * freqs * 128 * 1024 * 256
    residual, partial = pl.pallas_call(
        lambda *refs: forward_kernel(windows, *refs),
        out_shape=(
            jax.ShapeDtypeStruct(observed.shape, F32),
            jax.ShapeDtypeStruct((n_sta, count, windows, columns), F32),
        ),
        in_specs=[SMEM] + [VMEM] * 5,
        out_specs=(VMEM, VMEM),
        scratch_shapes=[
            pltpu.VMEM((blocks * windows, LANES), F32),
            pltpu.VMEM((classes * stations, freqs * LANES), F32),
            pltpu.VMEM((2, stations * freqs, LANES), F32),
            pltpu.VMEM((CHUNK * windows, LANES), F32),
        ],
        compiler_params=limit,
        cost_estimate=pl.CostEstimate(flops=flops, bytes_accessed=4 * 2**20, transcendentals=0),
    )(place, shards, green, pattern, observed, table)

    smooth = pl.pallas_call(
        lambda *refs: smooth_kernel(windows, *refs),
        out_shape=jax.ShapeDtypeStruct((count, windows, columns), F32),
        in_specs=[SMEM, SMEM, VMEM],
        out_specs=VMEM,
        compiler_params=limit,
        cost_estimate=pl.CostEstimate(flops=10**6, bytes_accessed=4 * 2**20, transcendentals=0),
    )(place, smooth_weight, shards)

    cores = [(0, 1), (1, 0)]
    mine = partial[0] + lax.ppermute(partial[1], "sta", cores)

    def across(value):
        return [
            lax.ppermute(value, "freq", [(i, i ^ k) for i in range(n_freq)])
            for k in range(1, n_freq)
        ]

    if n_freq <= 8:
        mine = sum(across(mine), mine) + smooth
    else:
        mine = lax.psum(mine, "freq") + smooth
    other = lax.ppermute(mine, "sta", cores)

    own, sums = pl.pallas_call(
        image_kernel,
        out_shape=(
            jax.ShapeDtypeStruct(slip.shape, F32),
            jax.ShapeDtypeStruct((2, 8, LANES), F32),
        ),
        in_specs=[SMEM] + [VMEM] * 5,
        out_specs=(VMEM, VMEM),
        scratch_shapes=[
            pltpu.VMEM((blocks * windows, LANES), F32),
            pltpu.VMEM((classes * stations, freqs * LANES), F32),
        ],
        compiler_params=limit,
        cost_estimate=pl.CostEstimate(flops=flops, bytes_accessed=4 * 2**20, transcendentals=0),
    )(place, mine, other, green, pattern, table)

    image = sums[0] + lax.ppermute(sums[0], "sta", cores)
    if n_freq <= 8:
        others = across(image)
    else:
        image, others = lax.psum(image, "freq"), []
    sums = jnp.stack([image, sums[1]])
    new_slip = pl.pallas_call(
        lambda *refs: update_kernel(len(others), *refs),
        out_shape=jax.ShapeDtypeStruct(slip.shape, F32),
        in_specs=[SMEM] + [VMEM] * (3 + len(others)),
        out_specs=VMEM,
    )(smooth_weight, sums, *others, slip, own)
    return new_slip, residual


def solution(mesh):
    n_freq = mesh.shape["freq"]
    placed = (
        P(None, ("grp", "freq", "tri")),
        P("freq", None, None, None),
        P("sta", None),
        P(None, ("grp", "freq"), "sta"),
        P(None, ("freq", "tri")),
        P("grp"),
    )

    def step(slip, green, pattern, observed, adjacency, smooth_weight):
        windows, block = slip.shape[0], green.shape[2]
        table = phase_table(green.shape[0] // n_freq * n_freq, windows, block)

        def body(*args):
            return local(*args, table=jnp.asarray(table))

        return jax.shard_map(
            body,
            mesh=mesh,
            in_specs=placed,
            out_specs=(P(None, ("grp", "freq", "tri")), P(None, ("grp", "freq"), "sta")),
            check_vma=False,
        )(slip, green, pattern, observed, adjacency, smooth_weight)

    return step
```

```python
import math

import jax
import jax.numpy as jnp
import numpy as np
from jax import lax
from jax.experimental import pallas as pl
from jax.experimental.pallas import tpu as pltpu
from jax.sharding import PartitionSpec as P

F32 = jnp.float32
BF16 = jnp.bfloat16
LANES = 128
CHUNK = 64


def phase_table(freq_total, windows, block):
    frequency = np.arange(freq_total, dtype=np.float32) + np.float32(1.0)
    window = np.arange(windows, dtype=np.float32) + np.float32(0.5)
    phases = np.float32(4.0 * math.pi / freq_total) * frequency[:, None] * window[None, :]
    phases = phases.astype(np.float64)
    both = np.stack([np.cos(phases), -np.sin(phases)], axis=-1).astype(np.float32)
    return np.repeat(both, block, axis=-1)


def split(value):
    high = value.astype(BF16)
    return high, (value - high.astype(F32)).astype(BF16)


def low_lanes(shape, block):
    return lax.broadcasted_iota(jnp.int32, shape, len(shape) - 1) < block


def spread_columns(read, parts, spread):
    def one(p, carry):
        value = read(p)
        for j in range(value.shape[1] // LANES):
            piece = value[:, j * LANES : (j + 1) * LANES]
            turned = pltpu.roll(piece, LANES // 2, 1)
            low = low_lanes(piece.shape, LANES // 2)
            row = (p * (value.shape[1] // LANES) + j) * 16
            row = row if isinstance(row, int) else pl.multiple_of(row, 16)
            spread[pl.ds(row, 8), :] = jnp.where(low, piece, turned)
            spread[pl.ds(row + 8, 8), :] = jnp.where(low, turned, piece)
        return carry

    if parts <= 8:
        for p in range(parts):
            one(p, 0)
    else:
        lax.fori_loop(0, parts, one, 0)


def onehot_of(pattern, classes):
    doubled = jnp.concatenate([pattern, pattern], axis=1)
    return jnp.concatenate([(doubled == k).astype(F32) for k in range(classes)], axis=0)


def over_chunks(count, step):
    if count == 1:
        step(0)
    else:
        lax.fori_loop(0, count, lambda n, carry: (step(n), carry)[1], 0)


def pack_kernel(slip, adjacency, out, held, sems):
    windows, columns = slip.shape
    neighbours, triangles = adjacency.shape
    copies = [
        pltpu.make_async_copy(adjacency, held, sems.at[0]),
        pltpu.make_async_copy(slip, out.at[:, pl.ds(0, columns)], sems.at[1]),
    ]
    for copy in copies:
        copy.start()
    copies[0].wait()
    out[:neighbours, columns:] = held[...].astype(F32)
    out[neighbours:, columns:] = jnp.zeros((windows - neighbours, triangles), F32)
    copies[1].wait()


def prepare_kernel(
    place,
    green_hbm,
    pattern_hbm,
    observed_hbm,
    table_hbm,
    green_out,
    onehot_out,
    turned_out,
    apart,
    table_out,
    green_ref,
    pattern_ref,
    observed,
    green_sems,
    sems,
):
    freqs, classes, block, _ = green_ref.shape
    chunks, stations, _ = pattern_ref.shape
    first = place[0] * freqs
    copies = [
        pltpu.make_async_copy(pattern_hbm, pattern_ref, sems.at[0]),
        pltpu.make_async_copy(observed_hbm, observed, sems.at[1]),
        pltpu.make_async_copy(table_hbm.at[pl.ds(first, freqs)], table_out, sems.at[2]),
    ]
    greens = [
        pltpu.make_async_copy(green_hbm.at[f], green_ref.at[f], green_sems.at[f])
        for f in range(freqs)
    ]
    for copy in copies + greens:
        copy.start()
    copies[0].wait()

    def step(n):
        onehot = onehot_of(pattern_ref[n], classes)
        onehot_out[n] = onehot.astype(BF16)
        turned = onehot[:, :block].T.astype(BF16)
        turned_out[n] = jnp.concatenate([turned, turned], axis=1)

    over_chunks(chunks, step)
    copies[1].wait()
    for r in range(2):
        for j in range(stations // 2):
            piece = observed[r, :, j * LANES : (j + 1) * LANES]
            apart[r, 2 * j * freqs : (2 * j + 1) * freqs, :] = piece
            apart[r, (2 * j + 1) * freqs : (2 * j + 2) * freqs, :] = pltpu.roll(piece, block, 1)
    copies[2].wait()
    for f in range(freqs):
        greens[f].wait()
        for k in range(classes):
            high, low = split(green_ref[f, k])
            green_out[f, :block, k * LANES : (k + 1) * LANES] = high
            green_out[f, block:, k * LANES : (k + 1) * LANES] = low


def pattern_sums(spread, table, onehot_ref, summed):
    freqs, windows, _ = table.shape
    chunks = onehot_ref.shape[0]

    def step(n):
        base = n * CHUNK * windows
        fields = [spread[pl.ds(base + w, CHUNK, stride=windows), :] for w in range(windows)]
        spectra = []
        for f in range(freqs):
            total = table[f, 0:1] * fields[0]
            for w in range(1, windows):
                total = total + table[f, w : w + 1] * fields[w]
            spectra.append(jnp.concatenate(split(total), axis=0))
        product = jnp.dot(
            onehot_ref[n], jnp.concatenate(spectra, axis=1), preferred_element_type=F32
        )
        if chunks == 1:
            summed[...] = product
        else:
            summed[...] += product

    if chunks > 1:
        summed[...] = jnp.zeros_like(summed)
    over_chunks(chunks, step)


def predict_one(summed, green, f, stations, block):
    value = summed[:, f * LANES : (f + 1) * LANES]
    sign = jnp.where(low_lanes(value.shape, block), 1.0, -1.0)
    real = value * sign
    imag = pltpu.roll(value, block, 1)
    classes = value.shape[0] // stations
    rows = []
    for half in zip(split(real), split(imag)):
        for part in half:
            rows.append(
                jnp.concatenate(
                    [part[k * stations : (k + 1) * stations] for k in range(classes)], axis=1
                )
            )
    left = jnp.concatenate(rows, axis=0)
    out = lax.dot_general(left, green, (((1,), (1,)), ((), ())), preferred_element_type=F32)
    high = out[: 2 * stations]
    low = out[2 * stations :]
    total = high + jnp.where(low_lanes(low.shape, block), low, 0.0)
    return total + pltpu.roll(total, block, 1)


def forward_kernel(windows, codes, place, *refs):
    count = max(len(codes), 1)
    pieces, refs = refs[:count], refs[count:]
    green, onehot_ref, turned_ref, apart, table = refs[:5]
    residual_out, partial_out = refs[5:7]
    if codes:
        shards, refs = refs[7], refs[8:]
        for (even, odd), piece in zip(codes, pieces):
            code = jnp.where(place[2] == 0, even, odd)
            shards[lax.bitwise_xor(place[1], code)] = piece[...]
    else:
        shards, refs = pieces[0], refs[7:]
    spread, summed, adjoint_rows, missed, fields = refs
    freqs, rows, _ = green.shape
    block = rows // 2
    stations = apart.shape[1] // freqs
    classes = summed.shape[0] // stations
    parts = shards.shape[0]
    half = place[2]
    width = partial_out.shape[3]
    low8 = low_lanes((freqs, LANES), block)
    spread_columns(lambda p: shards[p, :, :width], parts, spread)
    pattern_sums(spread, table, onehot_ref, summed)
    predicted = [predict_one(summed, green[f], f, stations, block) for f in range(freqs)]
    lefts = []
    for f in range(freqs):
        seen = jnp.concatenate(
            [apart[r, pl.ds(f, stations, stride=freqs), :] for r in range(2)], axis=0
        )
        misfit = predicted[f] - seen
        for r in range(2):
            missed[r, pl.ds(f, stations, stride=freqs), :] = misfit[r * stations : (r + 1) * stations]
        low = low_lanes(misfit.shape, block)
        misfit = jnp.where(low, misfit, pltpu.roll(misfit, block, 1))
        high, rest = split(misfit)
        lefts.append(jnp.concatenate([high, rest[:, :block]], axis=1))
    sign = jnp.where(low_lanes((stations, LANES), block), 1.0, -1.0)
    for f in range(freqs):
        right = jnp.concatenate([green[f], green[f, :block]], axis=0)
        out = jnp.dot(lefts[f], right, preferred_element_type=F32)
        at = slice(f * LANES, (f + 1) * LANES)
        for k in range(classes):
            real = out[:stations, k * LANES : (k + 1) * LANES]
            imag = out[stations:, k * LANES : (k + 1) * LANES]
            high, rest = split(real * sign + pltpu.roll(imag, block, 1))
            adjoint_rows[k * stations : (k + 1) * stations, at] = high
            adjoint_rows[(classes + k) * stations : (classes + k + 1) * stations, at] = rest
    for r in range(2):
        for j in range(stations // 2):
            even = missed[r, 2 * j * freqs : (2 * j + 1) * freqs, :]
            odd = missed[r, (2 * j + 1) * freqs : (2 * j + 2) * freqs, :]
            residual_out[r, :, j * LANES : (j + 1) * LANES] = jnp.where(
                low8, even, pltpu.roll(odd, block, 1)
            )

    per_part = width // block
    chunk_parts = CHUNK // per_part

    def step(n):
        adjoint = jnp.dot(turned_ref[n], adjoint_rows[...], preferred_element_type=F32)
        for w in range(windows):
            total = table[0, w : w + 1, :] * adjoint[:, :LANES]
            for f in range(1, freqs):
                total = total + table[f, w : w + 1, :] * adjoint[:, f * LANES : (f + 1) * LANES]
            fields[pl.ds(w, CHUNK, stride=windows), :] = total + pltpu.roll(total, block, 1)
        for q in range(chunk_parts):
            p = n * chunk_parts + q
            side = lax.rem(p // (parts // 2) + half, 2)
            slot = lax.rem(jnp.asarray(p, jnp.int32), parts // 2)
            for j in range(per_part // 2):
                row = (q * per_part + 2 * j) * windows
                partial_out[side, slot, :, j * LANES : (j + 1) * LANES] = jnp.where(
                    low8, fields[row : row + windows, :], fields[row + windows : row + 2 * windows, :]
                )

    over_chunks(turned_ref.shape[0], step)


def smooth_kernel(place, weight, shards, out):
    count, windows, width = out.shape
    parts = shards.shape[0]
    pieces = width // LANES
    lane = lax.broadcasted_iota(jnp.int32, (windows, LANES), 1)

    def pick(source, index):
        return jnp.take_along_axis(source, index, axis=1, mode="promise_in_bounds")

    def one(slot, carry):
        p = place[2] * count + slot
        around = [jnp.maximum(p - 1, 0), p, jnp.minimum(p + 1, parts - 1)]
        source = [shards[a, :, j * LANES : (j + 1) * LANES] for a in around for j in range(pieces)]
        for q in range(pieces):
            total = None
            for j in range(3):
                start = width + (q // 2) * LANES
                row = shards[p, j : j + 1, start : start + LANES]
                row = jnp.broadcast_to(row, (windows, LANES))
                target = pick(row, (q % 2) * (LANES // 2) + lane // 2).astype(jnp.int32)
                column = 2 * target + lane % 2 - (p - 1) * width
                inside = jnp.bitwise_and(column, LANES - 1)
                which = jnp.right_shift(column, 7)
                value = jnp.zeros((windows, LANES), F32)
                for v in range(q, q + 2 * pieces + 1):
                    value = jnp.where(which == v, pick(source[v], inside), value)
                total = value if total is None else total + value
            own = source[pieces + q]
            out[slot, :, q * LANES : (q + 1) * LANES] = weight[0] * (own - total / 3.0)
        return carry

    lax.fori_loop(0, count, one, 0)


def image_kernel(
    place, mine, other, green, onehot_ref, table, own_out, image_out, norm_out, spread, summed
):
    freqs, rows, _ = green.shape
    block = rows // 2
    classes = green.shape[2] // LANES
    stations = summed.shape[0] // classes
    count, windows, width = mine.shape
    half = place[2]

    def read(p):
        slot = p % count if isinstance(p, int) else lax.rem(p, count)
        return jnp.where(p // count == half, mine[slot], other[slot])

    spread_columns(read, 2 * count, spread)
    pattern_sums(spread, table, onehot_ref, summed)
    me = place[1]
    slot = lax.rem(me, count)
    own_out[...] = jnp.where(me // count == half, mine[slot], other[slot])

    def squares(p, total):
        value = read(p)
        value = value * value
        for j in range(width // LANES):
            total = total + value[:, j * LANES : (j + 1) * LANES]
        return total

    numerator = jnp.zeros((windows, LANES), F32)
    if count <= 4:
        for p in range(2 * count):
            numerator = squares(p, numerator)
    else:
        numerator = lax.fori_loop(0, 2 * count, squares, numerator)
    image = jnp.zeros((8, LANES), F32)
    for f in range(freqs):
        predicted = predict_one(summed, green[f], f, stations, block)
        predicted = predicted * predicted
        for j in range(predicted.shape[0] // 8):
            image = image + predicted[8 * j : 8 * j + 8]
    image = jnp.where(low_lanes(image.shape, block), image, 0.0)
    image_out[...] = jnp.broadcast_to(jnp.sum(image), image_out.shape)
    norm_out[...] = jnp.broadcast_to(jnp.sum(numerator), norm_out.shape)


SMEM = pl.BlockSpec(memory_space=pltpu.SMEM)
VMEM = pl.BlockSpec(memory_space=pltpu.VMEM)
HBM = pl.BlockSpec(memory_space=pltpu.HBM)


def local(slip, green, pattern, observed, adjacency, smooth_weight, *, table):
    n_freq, n_tri, n_sta = (lax.axis_size(a) for a in ("freq", "tri", "sta"))
    parts = n_freq * n_tri
    count = parts // n_sta
    freqs, classes, block, _ = green.shape
    windows, columns = slip.shape
    stations, blocks = pattern.shape
    index = [lax.axis_index(a) for a in (("freq",), ("freq", "tri"), ("sta",))]
    place = jnp.stack(index).astype(jnp.int32)
    pattern = pattern.reshape(stations, blocks // CHUNK, CHUNK).transpose(1, 0, 2)
    chunks = blocks // CHUNK
    grant = pltpu.CompilerParams(vmem_limit_bytes=(16 if chunks == 1 else 48) * 2**20)
    cores = [(0, 1), (1, 0)]
    shape = jax.ShapeDtypeStruct

    def across(value):
        return [
            lax.ppermute(value, "freq", [(i, i ^ k) for i in range(n_freq)])
            for k in range(1, n_freq)
        ]

    prepared = pl.pallas_call(
        prepare_kernel,
        out_shape=(
            shape((freqs, 2 * block, classes * 2 * block), BF16),
            shape((chunks, classes * stations, 2 * CHUNK), BF16),
            shape((chunks, CHUNK, 2 * classes * stations), BF16),
            shape((2, stations * freqs, LANES), F32),
            shape((freqs, windows, LANES), F32),
        ),
        in_specs=[SMEM] + [HBM] * 4,
        out_specs=(VMEM,) * 5,
        scratch_shapes=[
            pltpu.VMEM(green.shape, F32),
            pltpu.VMEM(pattern.shape, jnp.int32),
            pltpu.VMEM(observed.shape, F32),
            pltpu.SemaphoreType.DMA((freqs,)),
            pltpu.SemaphoreType.DMA((3,)),
        ],
        compiler_params=grant,
        cost_estimate=pl.CostEstimate(flops=10**6, bytes_accessed=6 * 2**20, transcendentals=0),
    )(place, green, pattern, observed, table)

    packed = pl.pallas_call(
        pack_kernel,
        out_shape=shape((windows, columns + adjacency.shape[1]), F32),
        in_specs=[HBM, HBM],
        out_specs=VMEM,
        scratch_shapes=[pltpu.VMEM(adjacency.shape, jnp.int32), pltpu.SemaphoreType.DMA((2,))],
        compiler_params=grant,
        cost_estimate=pl.CostEstimate(flops=10**10, bytes_accessed=2**16, transcendentals=0),
    )(slip, adjacency)
    if (n_freq, n_tri, n_sta) == (4, 2, 2):
        pieces = [packed, lax.ppermute(packed, "tri", cores)]
        codes = [(0, 0), (1, 1)]
        fetched = []
        for k in range(1, n_freq):
            pairs = [
                (4 * (z ^ k) + 2 * (t ^ s) + s, 4 * z + 2 * t + s)
                for z in range(n_freq)
                for t in range(n_tri)
                for s in range(n_sta)
            ]
            fetched.append(lax.ppermute(packed, ("freq", "tri", "sta"), pairs))
            codes.append((2 * k, 2 * k + 1))
        fetched, prepared = lax.optimization_barrier((fetched, prepared))
        pieces += fetched + [lax.ppermute(v, "sta", cores) for v in fetched]
        codes += [(2 * k + 1, 2 * k) for k in range(1, n_freq)]
    else:
        copies = jnp.broadcast_to(packed[None], (parts,) + packed.shape)
        pieces = [lax.all_to_all(copies, ("freq", "tri"), 0, 0, tiled=True)]
        codes = []

    pieces_of_green, onehot, turned, apart, own_table = prepared
    flops = 2 * freqs * 128 * 1024 * 256
    whole = shape((parts,) + packed.shape, F32)
    outs = pl.pallas_call(
        lambda *refs: forward_kernel(windows, codes, *refs),
        out_shape=(
            shape(observed.shape, F32),
            shape((n_sta, count, windows, columns), F32),
        )
        + ((whole,) if codes else ()),
        in_specs=[SMEM] + [VMEM] * (len(pieces) + 5),
        out_specs=(VMEM,) * (3 if codes else 2),
        scratch_shapes=[
            pltpu.VMEM((blocks * windows, LANES), F32),
            pltpu.VMEM((classes * stations, freqs * LANES), F32),
            pltpu.VMEM((2 * classes * stations, freqs * LANES), BF16),
            pltpu.VMEM((2, stations * freqs, LANES), F32),
            pltpu.VMEM((CHUNK * windows, LANES), F32),
        ],
        compiler_params=grant,
        cost_estimate=pl.CostEstimate(flops=flops, bytes_accessed=4 * 2**20, transcendentals=0),
    )(place, *pieces, pieces_of_green, onehot, turned, apart, own_table)
    residual, partial = outs[:2]
    shards = outs[2] if codes else pieces[0]

    smooth = pl.pallas_call(
        smooth_kernel,
        out_shape=shape((count, windows, columns), F32),
        in_specs=[SMEM, SMEM, VMEM],
        out_specs=VMEM,
        compiler_params=grant,
        cost_estimate=pl.CostEstimate(flops=10**6, bytes_accessed=4 * 2**20, transcendentals=0),
    )(place, smooth_weight, shards)

    mine = partial[0] + lax.ppermute(partial[1], "sta", cores)
    mine = sum(across(mine), mine) if n_freq <= 8 else lax.psum(mine, "freq")
    mine = mine + smooth
    other = lax.ppermute(mine, "sta", cores)

    own, image, numerator = pl.pallas_call(
        image_kernel,
        out_shape=(shape(slip.shape, F32),) * 3,
        in_specs=[SMEM] + [VMEM] * 5,
        out_specs=(VMEM,) * 3,
        scratch_shapes=[
            pltpu.VMEM((blocks * windows, LANES), F32),
            pltpu.VMEM((classes * stations, freqs * LANES), F32),
        ],
        compiler_params=grant,
        cost_estimate=pl.CostEstimate(flops=flops, bytes_accessed=4 * 2**20, transcendentals=0),
    )(place, mine, other, pieces_of_green, onehot, own_table)

    image = image + lax.ppermute(image, "sta", cores)
    image = sum(across(image), image) if n_freq <= 8 else lax.psum(image, "freq")
    step = numerator / (image + smooth_weight[0] * numerator)
    return jnp.maximum(slip - step * own, 0.0), residual


def solution(mesh):
    n_freq = mesh.shape["freq"]
    placed = (
        P(None, ("grp", "freq", "tri")),
        P("freq", None, None, None),
        P("sta", None),
        P(None, ("grp", "freq"), "sta"),
        P(None, ("freq", "tri")),
        P("grp"),
    )

    def step(slip, green, pattern, observed, adjacency, smooth_weight):
        windows, block = slip.shape[0], green.shape[2]
        table = phase_table(green.shape[0] // n_freq * n_freq, windows, block)

        def body(*args):
            return local(*args, table=jnp.asarray(table))

        return jax.shard_map(
            body,
            mesh=mesh,
            in_specs=placed,
            out_specs=(P(None, ("grp", "freq", "tri")), P(None, ("grp", "freq"), "sta")),
            check_vma=False,
        )(slip, green, pattern, observed, adjacency, smooth_weight)

    return step
```

```python
import math

import jax
import jax.numpy as jnp
import numpy as np
from jax import lax
from jax.experimental import pallas as pl
from jax.experimental.pallas import tpu as pltpu
from jax.sharding import PartitionSpec as P

F32 = jnp.float32
BF16 = jnp.bfloat16
LANES = 128
CHUNK = 64


def phase_table(freq_total, windows, block):
    frequency = np.arange(freq_total, dtype=np.float32) + np.float32(1.0)
    window = np.arange(windows, dtype=np.float32) + np.float32(0.5)
    phases = np.float32(4.0 * math.pi / freq_total) * frequency[:, None] * window[None, :]
    phases = phases.astype(np.float64)
    both = np.stack([np.cos(phases), -np.sin(phases)], axis=-1).astype(np.float32)
    return np.repeat(both, block, axis=-1)


def split(value):
    high = value.astype(BF16)
    return high, (value - high.astype(F32)).astype(BF16)


def low_lanes(shape, block):
    return lax.broadcasted_iota(jnp.int32, shape, len(shape) - 1) < block


def spread_columns(read, parts, spread):
    def one(p, carry):
        value = read(p)
        for j in range(value.shape[1] // LANES):
            piece = value[:, j * LANES : (j + 1) * LANES]
            turned = pltpu.roll(piece, LANES // 2, 1)
            low = low_lanes(piece.shape, LANES // 2)
            row = (p * (value.shape[1] // LANES) + j) * 16
            row = row if isinstance(row, int) else pl.multiple_of(row, 16)
            spread[pl.ds(row, 8), :] = jnp.where(low, piece, turned)
            spread[pl.ds(row + 8, 8), :] = jnp.where(low, turned, piece)
        return carry

    if parts <= 8:
        for p in range(parts):
            one(p, 0)
    else:
        lax.fori_loop(0, parts, one, 0)


def onehot_of(doubled, classes):
    return jnp.concatenate([(doubled == k).astype(F32) for k in range(classes)], axis=0)


def over_chunks(count, step):
    if count == 1:
        step(0)
    else:
        lax.fori_loop(0, count, lambda n, carry: (step(n), carry)[1], 0)


def positions():
    freq = lax.axis_index("freq")
    return freq, freq * lax.axis_size("tri") + lax.axis_index("tri"), lax.axis_index("sta")


def doubled_kernel(pattern, out):
    out[...] = jnp.concatenate([pattern[...], pattern[...]], axis=2)


def prepare_kernel(
    green_ref, pattern_ref, observed, table, green_out, onehot_out, turned_out, apart, table_out
):
    freqs, classes, block, _ = green_ref.shape
    chunks, stations, _ = pattern_ref.shape
    first = positions()[0] * freqs
    for f in range(freqs):
        for k in range(classes):
            high, low = split(green_ref[f, k])
            green_out[f, :block, k * LANES : (k + 1) * LANES] = high
            green_out[f, block:, k * LANES : (k + 1) * LANES] = low
        table_out[f] = table[first + f]

    def step(n):
        onehot = onehot_of(pattern_ref[n], classes)
        onehot_out[n] = onehot.astype(BF16)
        turned = onehot[:, :block].T.astype(BF16)
        turned_out[n] = jnp.concatenate([turned, turned], axis=1)

    over_chunks(chunks, step)
    for r in range(2):
        for j in range(stations // 2):
            piece = observed[r, :, j * LANES : (j + 1) * LANES]
            apart[r, 2 * j * freqs : (2 * j + 1) * freqs, :] = piece
            apart[r, (2 * j + 1) * freqs : (2 * j + 2) * freqs, :] = pltpu.roll(piece, block, 1)


def pattern_sums(spread, table, onehot_ref, summed):
    freqs, windows, _ = table.shape
    chunks = onehot_ref.shape[0]

    def step(n):
        base = n * CHUNK * windows
        fields = [spread[pl.ds(base + w, CHUNK, stride=windows), :] for w in range(windows)]
        spectra = []
        for f in range(freqs):
            total = table[f, 0:1] * fields[0]
            for w in range(1, windows):
                total = total + table[f, w : w + 1] * fields[w]
            spectra.append(jnp.concatenate(split(total), axis=0))
        product = jnp.dot(
            onehot_ref[n], jnp.concatenate(spectra, axis=1), preferred_element_type=F32
        )
        if chunks == 1:
            summed[...] = product
        else:
            summed[...] += product

    if chunks > 1:
        summed[...] = jnp.zeros_like(summed)
    over_chunks(chunks, step)


def predict_one(summed, green, f, stations, block):
    value = summed[:, f * LANES : (f + 1) * LANES]
    sign = jnp.where(low_lanes(value.shape, block), 1.0, -1.0)
    real = value * sign
    imag = pltpu.roll(value, block, 1)
    classes = value.shape[0] // stations
    rows = []
    for half in zip(split(real), split(imag)):
        for part in half:
            rows.append(
                jnp.concatenate(
                    [part[k * stations : (k + 1) * stations] for k in range(classes)], axis=1
                )
            )
    left = jnp.concatenate(rows, axis=0)
    out = lax.dot_general(left, green, (((1,), (1,)), ((), ())), preferred_element_type=F32)
    high = out[: 2 * stations]
    low = out[2 * stations :]
    total = high + jnp.where(low_lanes(low.shape, block), low, 0.0)
    return total + pltpu.roll(total, block, 1)


def forward_kernel(windows, codes, *refs):
    _, me, half = positions()
    count = max(len(codes), 1)
    pieces, refs = refs[:count], refs[count:]
    green, onehot_ref, turned_ref, apart, table = refs[:5]
    residual_out, partial_out = refs[5:7]
    if codes:
        shards, refs = refs[7], refs[8:]
        for (even, odd), piece in zip(codes, pieces):
            code = jnp.where(half == 0, even, odd).astype(jnp.int32)
            shards[lax.bitwise_xor(me, code)] = piece[...]
    else:
        shards, refs = pieces[0], refs[7:]
    spread, summed, adjoint_rows, missed, fields = refs
    freqs, rows, _ = green.shape
    block = rows // 2
    stations = apart.shape[1] // freqs
    classes = summed.shape[0] // stations
    parts = shards.shape[0]
    width = partial_out.shape[3]
    low8 = low_lanes((freqs, LANES), block)
    spread_columns(lambda p: shards[p], parts, spread)
    pattern_sums(spread, table, onehot_ref, summed)
    predicted = [predict_one(summed, green[f], f, stations, block) for f in range(freqs)]
    lefts = []
    for f in range(freqs):
        seen = jnp.concatenate(
            [apart[r, pl.ds(f, stations, stride=freqs), :] for r in range(2)], axis=0
        )
        misfit = predicted[f] - seen
        for r in range(2):
            missed[r, pl.ds(f, stations, stride=freqs), :] = misfit[r * stations : (r + 1) * stations]
        low = low_lanes(misfit.shape, block)
        misfit = jnp.where(low, misfit, pltpu.roll(misfit, block, 1))
        high, rest = split(misfit)
        lefts.append(jnp.concatenate([high, rest[:, :block]], axis=1))
    sign = jnp.where(low_lanes((stations, LANES), block), 1.0, -1.0)
    for f in range(freqs):
        right = jnp.concatenate([green[f], green[f, :block]], axis=0)
        out = jnp.dot(lefts[f], right, preferred_element_type=F32)
        at = slice(f * LANES, (f + 1) * LANES)
        for k in range(classes):
            real = out[:stations, k * LANES : (k + 1) * LANES]
            imag = out[stations:, k * LANES : (k + 1) * LANES]
            high, rest = split(real * sign + pltpu.roll(imag, block, 1))
            adjoint_rows[k * stations : (k + 1) * stations, at] = high
            adjoint_rows[(classes + k) * stations : (classes + k + 1) * stations, at] = rest
    for r in range(2):
        for j in range(stations // 2):
            even = missed[r, 2 * j * freqs : (2 * j + 1) * freqs, :]
            odd = missed[r, (2 * j + 1) * freqs : (2 * j + 2) * freqs, :]
            residual_out[r, :, j * LANES : (j + 1) * LANES] = jnp.where(
                low8, even, pltpu.roll(odd, block, 1)
            )

    per_part = width // block
    chunk_parts = CHUNK // per_part

    def step(n):
        adjoint = jnp.dot(turned_ref[n], adjoint_rows[...], preferred_element_type=F32)
        for w in range(windows):
            total = table[0, w : w + 1, :] * adjoint[:, :LANES]
            for f in range(1, freqs):
                total = total + table[f, w : w + 1, :] * adjoint[:, f * LANES : (f + 1) * LANES]
            fields[pl.ds(w, CHUNK, stride=windows), :] = total + pltpu.roll(total, block, 1)
        for q in range(chunk_parts):
            p = n * chunk_parts + q
            side = lax.rem(p // (parts // 2) + half, 2)
            slot = lax.rem(jnp.asarray(p, jnp.int32), parts // 2)
            for j in range(per_part // 2):
                row = (q * per_part + 2 * j) * windows
                partial_out[side, slot, :, j * LANES : (j + 1) * LANES] = jnp.where(
                    low8, fields[row : row + windows, :], fields[row + windows : row + 2 * windows, :]
                )

    over_chunks(turned_ref.shape[0], step)


def smooth_kernel(shards, *refs):
    adjacency, out = refs[:-1], refs[-1]
    count, windows, width = out.shape
    parts = shards.shape[0]
    tris = len(adjacency)
    pieces = width // LANES
    lane = lax.broadcasted_iota(jnp.int32, (windows, LANES), 1)

    def pick(source, index):
        return jnp.take_along_axis(source, index, axis=1, mode="promise_in_bounds")

    out[...] = jnp.zeros(out.shape, F32)
    _, me, half = positions()
    for k in range(tris):
        p = me - lax.rem(me, tris) + lax.bitwise_xor(lax.rem(me, tris), jnp.int32(k))
        factor = jnp.where(p // count == half, 1.0, 0.0)
        around = [jnp.maximum(p - 1, 0), p, jnp.minimum(p + 1, parts - 1)]
        source = [shards[a, :, j * LANES : (j + 1) * LANES] for a in around for j in range(pieces)]
        for q in range(pieces):
            total = None
            for j in range(3):
                row = adjacency[k][j : j + 1, (q // 2) * LANES : (q // 2 + 1) * LANES]
                row = jnp.broadcast_to(row, (windows, LANES))
                target = pick(row, (q % 2) * (LANES // 2) + lane // 2)
                column = 2 * target + lane % 2 - (p - 1) * width
                inside = jnp.bitwise_and(column, LANES - 1)
                which = jnp.right_shift(column, 7)
                value = jnp.zeros((windows, LANES), F32)
                for v in range(q, q + 2 * pieces + 1):
                    value = jnp.where(which == v, pick(source[v], inside), value)
                total = value if total is None else total + value
            own = source[pieces + q]
            out[lax.rem(p, count), :, q * LANES : (q + 1) * LANES] = factor * (own - total / 3.0)


def image_kernel(
    mine, other, green, onehot_ref, table, weight, own_out, image_out, norm_out, spread, summed
):
    freqs, rows, _ = green.shape
    block = rows // 2
    classes = green.shape[2] // LANES
    stations = summed.shape[0] // classes
    count, windows, width = mine.shape
    _, me, half = positions()

    def read(p):
        slot = p % count if isinstance(p, int) else lax.rem(p, count)
        return jnp.where(p // count == half, mine[slot], other[slot])

    spread_columns(read, 2 * count, spread)
    pattern_sums(spread, table, onehot_ref, summed)
    slot = lax.rem(me, count)
    own_out[...] = jnp.where(me // count == half, mine[slot], other[slot])

    def squares(p, total):
        value = read(p)
        value = value * value
        for j in range(width // LANES):
            total = total + value[:, j * LANES : (j + 1) * LANES]
        return total

    numerator = jnp.zeros((windows, LANES), F32)
    if count <= 4:
        for p in range(2 * count):
            numerator = squares(p, numerator)
    else:
        numerator = lax.fori_loop(0, 2 * count, squares, numerator)
    image = jnp.zeros((8, LANES), F32)
    for f in range(freqs):
        predicted = predict_one(summed, green[f], f, stations, block)
        predicted = predicted * predicted
        for j in range(predicted.shape[0] // 8):
            image = image + predicted[8 * j : 8 * j + 8]
    image = jnp.where(low_lanes(image.shape, block), image, 0.0)
    image_out[...] = jnp.broadcast_to(jnp.sum(image), image_out.shape)
    norm_out[0] = jnp.broadcast_to(jnp.sum(numerator), norm_out.shape[1:])
    norm_out[1] = weight[...] * norm_out[0]


def update_kernel(images, norm, slip, own, out):
    image = images[0]
    for n in range(1, images.shape[0]):
        image = image + images[n]
    step = norm[0] / (image + norm[1])
    for j in range(slip.shape[1] // LANES):
        at = slice(j * LANES, (j + 1) * LANES)
        out[:, at] = jnp.maximum(slip[:, at] - step * own[:, at], 0.0)


VMEM = pl.BlockSpec(memory_space=pltpu.VMEM)


def local(slip, green, pattern, observed, adjacency, smooth_weight, *, table):
    n_freq, n_tri, n_sta = (lax.axis_size(a) for a in ("freq", "tri", "sta"))
    parts = n_freq * n_tri
    count = parts // n_sta
    freqs, classes, block, _ = green.shape
    windows, columns = slip.shape
    stations, blocks = pattern.shape
    pattern = pattern.reshape(stations, blocks // CHUNK, CHUNK).transpose(1, 0, 2)
    chunks = blocks // CHUNK
    grant = pltpu.CompilerParams(vmem_limit_bytes=(16 if chunks == 1 else 48) * 2**20)
    cores = [(0, 1), (1, 0)]
    shape = jax.ShapeDtypeStruct

    def across(value):
        return [
            lax.ppermute(value, "freq", [(i, i ^ k) for i in range(n_freq)])
            for k in range(1, n_freq)
        ]

    doubled = pl.pallas_call(
        doubled_kernel,
        out_shape=shape((chunks, stations, 2 * CHUNK), jnp.int32),
        in_specs=[VMEM],
        out_specs=VMEM,
        compiler_params=grant,
        cost_estimate=pl.CostEstimate(flops=10**10, bytes_accessed=2**10, transcendentals=0),
    )(pattern)
    prepared = pl.pallas_call(
        prepare_kernel,
        out_shape=(
            shape((freqs, 2 * block, classes * 2 * block), BF16),
            shape((chunks, classes * stations, 2 * CHUNK), BF16),
            shape((chunks, CHUNK, 2 * classes * stations), BF16),
            shape((2, stations * freqs, LANES), F32),
            shape((freqs, windows, LANES), F32),
        ),
        in_specs=[VMEM] * 4,
        out_specs=(VMEM,) * 5,
        compiler_params=grant,
        cost_estimate=pl.CostEstimate(flops=10**6, bytes_accessed=6 * 2**20, transcendentals=0),
    )(green, doubled, observed, table)
    neighbours = [adjacency] + [
        lax.ppermute(adjacency, "tri", [(i, i ^ k) for i in range(n_tri)]) for k in range(1, n_tri)
    ]
    if (n_freq, n_tri, n_sta) == (4, 2, 2):
        pieces = [slip, lax.ppermute(slip, "tri", cores)]
        codes = [(0, 0), (1, 1)]
        fetched = []
        for k in range(1, n_freq):
            pairs = [
                (4 * (z ^ k) + 2 * (t ^ s) + s, 4 * z + 2 * t + s)
                for z in range(n_freq)
                for t in range(n_tri)
                for s in range(n_sta)
            ]
            fetched.append(lax.ppermute(slip, ("freq", "tri", "sta"), pairs))
            codes.append((2 * k, 2 * k + 1))
        fetched[0], prepared = lax.optimization_barrier((fetched[0], prepared))
        fetched[-1], neighbours = lax.optimization_barrier((fetched[-1], neighbours))
        pieces += fetched + [lax.ppermute(v, "sta", cores) for v in fetched]
        codes += [(2 * k + 1, 2 * k) for k in range(1, n_freq)]
    else:
        copies = jnp.broadcast_to(slip[None], (parts,) + slip.shape)
        pieces = [lax.all_to_all(copies, ("freq", "tri"), 0, 0, tiled=True)]
        codes = []

    pieces_of_green, onehot, turned, apart, own_table = prepared
    flops = 2 * freqs * 128 * 1024 * 256
    whole = shape((parts,) + slip.shape, F32)
    outs = pl.pallas_call(
        lambda *refs: forward_kernel(windows, codes, *refs),
        out_shape=(
            shape(observed.shape, F32),
            shape((n_sta, count, windows, columns), F32),
        )
        + ((whole,) if codes else ()),
        in_specs=[VMEM] * (len(pieces) + 5),
        out_specs=(VMEM,) * (3 if codes else 2),
        scratch_shapes=[
            pltpu.VMEM((blocks * windows, LANES), F32),
            pltpu.VMEM((classes * stations, freqs * LANES), F32),
            pltpu.VMEM((2 * classes * stations, freqs * LANES), BF16),
            pltpu.VMEM((2, stations * freqs, LANES), F32),
            pltpu.VMEM((CHUNK * windows, LANES), F32),
        ],
        compiler_params=grant,
        cost_estimate=pl.CostEstimate(flops=flops, bytes_accessed=4 * 2**20, transcendentals=0),
    )(*pieces, pieces_of_green, onehot, turned, apart, own_table)
    residual, partial = outs[:2]
    shards = outs[2] if codes else pieces[0]

    smooth = pl.pallas_call(
        smooth_kernel,
        out_shape=shape((count, windows, columns), F32),
        in_specs=[VMEM] * (1 + n_tri),
        out_specs=VMEM,
        compiler_params=grant,
        cost_estimate=pl.CostEstimate(flops=10**6, bytes_accessed=4 * 2**20, transcendentals=0),
    )(shards, *neighbours)

    mine = partial[0] + lax.ppermute(partial[1], "sta", cores)
    mine = mine + smooth_weight[0] * smooth
    mine = sum(across(mine), mine) if n_freq <= 8 else lax.psum(mine, "freq")
    other = lax.ppermute(mine, "sta", cores)

    ranks = n_freq * n_sta
    own, image, norm = pl.pallas_call(
        image_kernel,
        out_shape=(
            shape(slip.shape, F32),
            shape((ranks, 8, LANES), F32),
            shape((2, 8, LANES), F32),
        ),
        in_specs=[VMEM] * 6,
        out_specs=(VMEM,) * 3,
        scratch_shapes=[
            pltpu.VMEM((blocks * windows, LANES), F32),
            pltpu.VMEM((classes * stations, freqs * LANES), F32),
        ],
        compiler_params=grant,
        cost_estimate=pl.CostEstimate(flops=flops, bytes_accessed=4 * 2**20, transcendentals=0),
    )(mine, other, pieces_of_green, onehot, own_table, smooth_weight.reshape(1, 1))

    images = lax.all_to_all(image, ("freq", "sta"), 0, 0, tiled=True)
    new_slip = pl.pallas_call(
        update_kernel,
        out_shape=shape(slip.shape, F32),
        in_specs=[VMEM] * 4,
        out_specs=VMEM,
        compiler_params=grant,
    )(images, norm, slip, own)
    return new_slip, residual


def solution(mesh):
    n_freq = mesh.shape["freq"]
    placed = (
        P(None, ("grp", "freq", "tri")),
        P("freq", None, None, None),
        P("sta", None),
        P(None, ("grp", "freq"), "sta"),
        P(None, ("freq", "tri")),
        P("grp"),
    )

    def step(slip, green, pattern, observed, adjacency, smooth_weight):
        windows, block = slip.shape[0], green.shape[2]
        table = phase_table(green.shape[0] // n_freq * n_freq, windows, block)

        def body(*args):
            return local(*args, table=jnp.asarray(table))

        return jax.shard_map(
            body,
            mesh=mesh,
            in_specs=placed,
            out_specs=(P(None, ("grp", "freq", "tri")), P(None, ("grp", "freq"), "sta")),
            check_vma=False,
        )(slip, green, pattern, observed, adjacency, smooth_weight)

    return step
```

```python
import math

import jax
import jax.numpy as jnp
import numpy as np
from jax import lax
from jax.experimental import pallas as pl
from jax.experimental.pallas import tpu as pltpu
from jax.sharding import PartitionSpec as P

F32 = jnp.float32
BF16 = jnp.bfloat16
LANES = 128
CHUNK = 64


def phase_table(freq_total, windows, block):
    frequency = np.arange(freq_total, dtype=np.float32) + np.float32(1.0)
    window = np.arange(windows, dtype=np.float32) + np.float32(0.5)
    phases = np.float32(4.0 * math.pi / freq_total) * frequency[:, None] * window[None, :]
    phases = phases.astype(np.float64)
    both = np.stack([np.cos(phases), -np.sin(phases)], axis=-1).astype(np.float32)
    return np.repeat(both, block, axis=-1)


def split(value):
    high = value.astype(BF16)
    return high, (value - high.astype(F32)).astype(BF16)


def low_lanes(shape, block):
    return lax.broadcasted_iota(jnp.int32, shape, len(shape) - 1) < block


def spread_columns(read, parts, spread):
    def one(p, carry):
        value = read(p)
        for j in range(value.shape[1] // LANES):
            piece = value[:, j * LANES : (j + 1) * LANES]
            turned = pltpu.roll(piece, LANES // 2, 1)
            low = low_lanes(piece.shape, LANES // 2)
            row = (p * (value.shape[1] // LANES) + j) * 16
            row = row if isinstance(row, int) else pl.multiple_of(row, 16)
            spread[pl.ds(row, 8), :] = jnp.where(low, piece, turned)
            spread[pl.ds(row + 8, 8), :] = jnp.where(low, turned, piece)
        return carry

    if parts <= 8:
        for p in range(parts):
            one(p, 0)
    else:
        lax.fori_loop(0, parts, one, 0)


def onehot_of(doubled, classes):
    return jnp.concatenate([(doubled == k).astype(F32) for k in range(classes)], axis=0)


def over_chunks(count, step):
    if count == 1:
        step(0)
    else:
        lax.fori_loop(0, count, lambda n, carry: (step(n), carry)[1], 0)


def positions():
    freq = lax.axis_index("freq")
    return freq, freq * lax.axis_size("tri") + lax.axis_index("tri"), lax.axis_index("sta")


def ahead_kernel(out):
    out[...] = jnp.zeros(out.shape, F32)


def pack_kernel(slip, adjacency, out):
    windows, columns = slip.shape
    neighbours, triangles = adjacency.shape
    out[:, :columns] = slip[...]
    out[:neighbours, columns:] = adjacency[...].astype(F32)
    out[neighbours:, columns:] = jnp.zeros((windows - neighbours, triangles), F32)


def prepare_kernel(
    green_ref,
    pattern_ref,
    observed,
    table,
    ahead,
    green_out,
    onehot_out,
    turned_out,
    apart,
    table_out,
    ahead_out,
):
    freqs, classes, block, _ = green_ref.shape
    chunks, stations, _ = pattern_ref.shape
    first = positions()[0] * freqs
    ahead_out[...] = ahead[...]
    for f in range(freqs):
        for k in range(classes):
            high, low = split(green_ref[f, k])
            green_out[f, :block, k * LANES : (k + 1) * LANES] = high
            green_out[f, block:, k * LANES : (k + 1) * LANES] = low
        table_out[f] = table[first + f]

    def step(n):
        value = pattern_ref[n]
        onehot = onehot_of(jnp.concatenate([value, value], axis=1), classes)
        onehot_out[n] = onehot.astype(BF16)
        turned = onehot[:, :block].T.astype(BF16)
        turned_out[n] = jnp.concatenate([turned, turned], axis=1)

    over_chunks(chunks, step)
    for r in range(2):
        for j in range(stations // 2):
            piece = observed[r, :, j * LANES : (j + 1) * LANES]
            apart[r, 2 * j * freqs : (2 * j + 1) * freqs, :] = piece
            apart[r, (2 * j + 1) * freqs : (2 * j + 2) * freqs, :] = pltpu.roll(piece, block, 1)


def pattern_sums(spread, table, onehot_ref, summed):
    freqs, windows, _ = table.shape
    chunks = onehot_ref.shape[0]

    def step(n):
        base = n * CHUNK * windows
        fields = [spread[pl.ds(base + w, CHUNK, stride=windows), :] for w in range(windows)]
        spectra = []
        for f in range(freqs):
            total = table[f, 0:1] * fields[0]
            for w in range(1, windows):
                total = total + table[f, w : w + 1] * fields[w]
            spectra.append(jnp.concatenate(split(total), axis=0))
        product = jnp.dot(
            onehot_ref[n], jnp.concatenate(spectra, axis=1), preferred_element_type=F32
        )
        if chunks == 1:
            summed[...] = product
        else:
            summed[...] += product

    if chunks > 1:
        summed[...] = jnp.zeros_like(summed)
    over_chunks(chunks, step)


def predict_one(summed, green, f, stations, block):
    value = summed[:, f * LANES : (f + 1) * LANES]
    sign = jnp.where(low_lanes(value.shape, block), 1.0, -1.0)
    real = value * sign
    imag = pltpu.roll(value, block, 1)
    classes = value.shape[0] // stations
    rows = []
    for half in zip(split(real), split(imag)):
        for part in half:
            rows.append(
                jnp.concatenate(
                    [part[k * stations : (k + 1) * stations] for k in range(classes)], axis=1
                )
            )
    left = jnp.concatenate(rows, axis=0)
    out = lax.dot_general(left, green, (((1,), (1,)), ((), ())), preferred_element_type=F32)
    high = out[: 2 * stations]
    low = out[2 * stations :]
    total = high + jnp.where(low_lanes(low.shape, block), low, 0.0)
    return total + pltpu.roll(total, block, 1)


def forward_kernel(windows, codes, *refs):
    _, me, half = positions()
    count = max(len(codes), 1)
    pieces, refs = refs[:count], refs[count:]
    green, onehot_ref, turned_ref, apart, table, ahead, weight = refs[:7]
    residual_out, partial_out, weight_out = refs[7:10]
    weight_out[...] = ahead[...] + weight[...]
    if codes:
        shards, refs = refs[10], refs[11:]
        for (even, odd), piece in zip(codes, pieces):
            code = jnp.where(half == 0, even, odd).astype(jnp.int32)
            shards[lax.bitwise_xor(me, code)] = piece[:, : shards.shape[2]]
    else:
        shards, refs = pieces[0], refs[10:]
    spread, summed, adjoint_rows, missed, fields = refs
    freqs, rows, _ = green.shape
    block = rows // 2
    stations = apart.shape[1] // freqs
    classes = summed.shape[0] // stations
    parts = shards.shape[0]
    width = partial_out.shape[3]
    low8 = low_lanes((freqs, LANES), block)
    spread_columns(lambda p: shards[p], parts, spread)
    pattern_sums(spread, table, onehot_ref, summed)
    predicted = [predict_one(summed, green[f], f, stations, block) for f in range(freqs)]
    lefts = []
    for f in range(freqs):
        seen = jnp.concatenate(
            [apart[r, pl.ds(f, stations, stride=freqs), :] for r in range(2)], axis=0
        )
        misfit = predicted[f] - seen
        for r in range(2):
            missed[r, pl.ds(f, stations, stride=freqs), :] = misfit[r * stations : (r + 1) * stations]
        low = low_lanes(misfit.shape, block)
        misfit = jnp.where(low, misfit, pltpu.roll(misfit, block, 1))
        high, rest = split(misfit)
        lefts.append(jnp.concatenate([high, rest[:, :block]], axis=1))
    sign = jnp.where(low_lanes((stations, LANES), block), 1.0, -1.0)
    for f in range(freqs):
        right = jnp.concatenate([green[f], green[f, :block]], axis=0)
        out = jnp.dot(lefts[f], right, preferred_element_type=F32)
        at = slice(f * LANES, (f + 1) * LANES)
        for k in range(classes):
            real = out[:stations, k * LANES : (k + 1) * LANES]
            imag = out[stations:, k * LANES : (k + 1) * LANES]
            high, rest = split(real * sign + pltpu.roll(imag, block, 1))
            adjoint_rows[k * stations : (k + 1) * stations, at] = high
            adjoint_rows[(classes + k) * stations : (classes + k + 1) * stations, at] = rest
    for r in range(2):
        for j in range(stations // 2):
            even = missed[r, 2 * j * freqs : (2 * j + 1) * freqs, :]
            odd = missed[r, (2 * j + 1) * freqs : (2 * j + 2) * freqs, :]
            residual_out[r, :, j * LANES : (j + 1) * LANES] = jnp.where(
                low8, even, pltpu.roll(odd, block, 1)
            )

    per_part = width // block
    chunk_parts = CHUNK // per_part

    def step(n):
        adjoint = jnp.dot(turned_ref[n], adjoint_rows[...], preferred_element_type=F32)
        for w in range(windows):
            total = table[0, w : w + 1, :] * adjoint[:, :LANES]
            for f in range(1, freqs):
                total = total + table[f, w : w + 1, :] * adjoint[:, f * LANES : (f + 1) * LANES]
            fields[pl.ds(w, CHUNK, stride=windows), :] = total + pltpu.roll(total, block, 1)
        for q in range(chunk_parts):
            p = n * chunk_parts + q
            side = lax.rem(p // (parts // 2) + half, 2)
            slot = lax.rem(jnp.asarray(p, jnp.int32), parts // 2)
            for j in range(per_part // 2):
                row = (q * per_part + 2 * j) * windows
                partial_out[side, slot, :, j * LANES : (j + 1) * LANES] = jnp.where(
                    low8, fields[row : row + windows, :], fields[row + windows : row + 2 * windows, :]
                )

    over_chunks(turned_ref.shape[0], step)


def smooth_kernel(shards, weight, *refs):
    adjacency, out = refs[:-1], refs[-1]
    count, windows, width = out.shape
    parts = shards.shape[0]
    tris = len(adjacency)
    pieces = width // LANES
    lane = lax.broadcasted_iota(jnp.int32, (windows, LANES), 1)

    def pick(source, index):
        return jnp.take_along_axis(source, index, axis=1, mode="promise_in_bounds")

    out[...] = jnp.zeros(out.shape, F32)
    _, me, half = positions()
    for k in range(tris):
        p = me - lax.rem(me, tris) + lax.bitwise_xor(lax.rem(me, tris), jnp.int32(k))
        factor = jnp.where(p // count == half, weight[...], 0.0)
        around = [jnp.maximum(p - 1, 0), p, jnp.minimum(p + 1, parts - 1)]
        source = [shards[a, :, j * LANES : (j + 1) * LANES] for a in around for j in range(pieces)]
        for q in range(pieces):
            for j in range(3):
                start = width + (q // 2) * LANES
                row = adjacency[k][j : j + 1, start : start + LANES]
                row = jnp.broadcast_to(row, (windows, LANES))
                target = pick(row, (q % 2) * (LANES // 2) + lane // 2).astype(jnp.int32)
                if j == 0:
                    total = jnp.where(target < p * (width // 2), source[q], source[2 * pieces + q])
                    continue
                column = 2 * target + lane % 2 - (p - 1) * width
                inside = jnp.bitwise_and(column, LANES - 1)
                which = jnp.right_shift(column, 7)
                value = jnp.zeros((windows, LANES), F32)
                for v in range(q, q + 2 * pieces + 1):
                    value = jnp.where(which == v, pick(source[v], inside), value)
                total = total + value
            own = source[pieces + q]
            out[lax.rem(p, count), :, q * LANES : (q + 1) * LANES] = factor * (own - total / 3.0)


def image_kernel(
    mine, other, green, onehot_ref, table, weight, own_out, image_out, norm_out, spread, summed
):
    freqs, rows, _ = green.shape
    block = rows // 2
    classes = green.shape[2] // LANES
    stations = summed.shape[0] // classes
    count, windows, width = mine.shape
    _, me, half = positions()

    def read(p):
        slot = p % count if isinstance(p, int) else lax.rem(p, count)
        return jnp.where(p // count == half, mine[slot], other[slot])

    spread_columns(read, 2 * count, spread)
    pattern_sums(spread, table, onehot_ref, summed)
    slot = lax.rem(me, count)
    own_out[...] = jnp.where(me // count == half, mine[slot], other[slot])

    def squares(p, total):
        value = read(p)
        value = value * value
        for j in range(width // LANES):
            total = total + value[:, j * LANES : (j + 1) * LANES]
        return total

    numerator = jnp.zeros((windows, LANES), F32)
    if count <= 4:
        for p in range(2 * count):
            numerator = squares(p, numerator)
    else:
        numerator = lax.fori_loop(0, 2 * count, squares, numerator)
    image = jnp.zeros((8, LANES), F32)
    for f in range(freqs):
        predicted = predict_one(summed, green[f], f, stations, block)
        predicted = predicted * predicted
        for j in range(predicted.shape[0] // 8):
            image = image + predicted[8 * j : 8 * j + 8]
    image = jnp.where(low_lanes(image.shape, block), image, 0.0)
    image_out[...] = jnp.broadcast_to(jnp.sum(image), image_out.shape)
    norm_out[0] = jnp.broadcast_to(jnp.sum(numerator), norm_out.shape[1:])
    norm_out[1] = weight[...] * norm_out[0]


def update_kernel(images, norm, slip, own, out):
    image = images[0]
    for n in range(1, images.shape[0]):
        image = image + images[n]
    step = norm[0] / (image + norm[1])
    for j in range(slip.shape[1] // LANES):
        at = slice(j * LANES, (j + 1) * LANES)
        out[:, at] = jnp.maximum(slip[:, at] - step * own[:, at], 0.0)


VMEM = pl.BlockSpec(memory_space=pltpu.VMEM)


def local(slip, green, pattern, observed, adjacency, smooth_weight, *, table):
    n_freq, n_tri, n_sta = (lax.axis_size(a) for a in ("freq", "tri", "sta"))
    parts = n_freq * n_tri
    count = parts // n_sta
    freqs, classes, block, _ = green.shape
    windows, columns = slip.shape
    stations, blocks = pattern.shape
    pattern = pattern.reshape(stations, blocks // CHUNK, CHUNK).transpose(1, 0, 2)
    chunks = blocks // CHUNK
    grant = pltpu.CompilerParams(vmem_limit_bytes=(16 if chunks == 1 else 48) * 2**20)
    cores = [(0, 1), (1, 0)]
    shape = jax.ShapeDtypeStruct

    def across(value):
        return [
            lax.ppermute(value, "freq", [(i, i ^ k) for i in range(n_freq)])
            for k in range(1, n_freq)
        ]

    ahead = pl.pallas_call(
        ahead_kernel,
        out_shape=shape((8, LANES), F32),
        out_specs=VMEM,
        compiler_params=grant,
        cost_estimate=pl.CostEstimate(flops=10**10, bytes_accessed=2**10, transcendentals=0),
    )()
    adjacency, ahead = lax.optimization_barrier((adjacency, ahead))
    prepared = pl.pallas_call(
        prepare_kernel,
        out_shape=(
            shape((freqs, 2 * block, classes * 2 * block), BF16),
            shape((chunks, classes * stations, 2 * CHUNK), BF16),
            shape((chunks, CHUNK, 2 * classes * stations), BF16),
            shape((2, stations * freqs, LANES), F32),
            shape((freqs, windows, LANES), F32),
            shape((8, LANES), F32),
        ),
        in_specs=[VMEM] * 5,
        out_specs=(VMEM,) * 6,
        compiler_params=grant,
        cost_estimate=pl.CostEstimate(flops=10**6, bytes_accessed=6 * 2**20, transcendentals=0),
    )(green, pattern, observed, table, ahead)
    packed = pl.pallas_call(
        pack_kernel,
        out_shape=shape((windows, columns + adjacency.shape[1]), F32),
        in_specs=[VMEM] * 2,
        out_specs=VMEM,
        compiler_params=grant,
    )(slip, adjacency)
    neighbours = [packed] + [
        lax.ppermute(packed, "tri", [(i, i ^ k) for i in range(n_tri)]) for k in range(1, n_tri)
    ]
    if (n_freq, n_tri, n_sta) == (4, 2, 2):
        pieces = list(neighbours)
        codes = [(0, 0), (1, 1)]
        fetched = []
        for k in range(1, n_freq):
            pairs = [
                (4 * (z ^ k) + 2 * (t ^ s) + s, 4 * z + 2 * t + s)
                for z in range(n_freq)
                for t in range(n_tri)
                for s in range(n_sta)
            ]
            fetched.append(lax.ppermute(slip, ("freq", "tri", "sta"), pairs))
            codes.append((2 * k, 2 * k + 1))
        fetched[0], prepared = lax.optimization_barrier((fetched[0], prepared))
        pieces += fetched + [lax.ppermute(v, "sta", cores) for v in fetched]
        codes += [(2 * k + 1, 2 * k) for k in range(1, n_freq)]
    else:
        copies = jnp.broadcast_to(slip[None], (parts,) + slip.shape)
        pieces = [lax.all_to_all(copies, ("freq", "tri"), 0, 0, tiled=True)]
        codes = []

    pieces_of_green, onehot, turned, apart, own_table, ahead = prepared
    flops = 2 * freqs * 128 * 1024 * 256
    whole = shape((parts,) + slip.shape, F32)
    outs = pl.pallas_call(
        lambda *refs: forward_kernel(windows, codes, *refs),
        out_shape=(
            shape(observed.shape, F32),
            shape((n_sta, count, windows, columns), F32),
            shape((8, LANES), F32),
        )
        + ((whole,) if codes else ()),
        in_specs=[VMEM] * (len(pieces) + 7),
        out_specs=(VMEM,) * (4 if codes else 3),
        scratch_shapes=[
            pltpu.VMEM((blocks * windows, LANES), F32),
            pltpu.VMEM((classes * stations, freqs * LANES), F32),
            pltpu.VMEM((2 * classes * stations, freqs * LANES), BF16),
            pltpu.VMEM((2, stations * freqs, LANES), F32),
            pltpu.VMEM((CHUNK * windows, LANES), F32),
        ],
        compiler_params=grant,
        cost_estimate=pl.CostEstimate(flops=flops, bytes_accessed=4 * 2**20, transcendentals=0),
    )(*pieces, pieces_of_green, onehot, turned, apart, own_table, ahead, smooth_weight.reshape(1, 1))
    residual, partial, weights = outs[:3]
    shards = outs[3] if codes else pieces[0]

    smooth = pl.pallas_call(
        smooth_kernel,
        out_shape=shape((count, windows, columns), F32),
        in_specs=[VMEM] * (2 + n_tri),
        out_specs=VMEM,
        compiler_params=grant,
        cost_estimate=pl.CostEstimate(flops=10**6, bytes_accessed=4 * 2**20, transcendentals=0),
    )(shards, weights, *neighbours)

    mine = partial[0] + lax.ppermute(partial[1], "sta", cores)
    mine = mine + smooth
    mine = sum(across(mine), mine) if n_freq <= 8 else lax.psum(mine, "freq")
    other = lax.ppermute(mine, "sta", cores)

    ranks = n_freq * n_sta
    own, image, norm = pl.pallas_call(
        image_kernel,
        out_shape=(
            shape(slip.shape, F32),
            shape((ranks, 8, LANES), F32),
            shape((2, 8, LANES), F32),
        ),
        in_specs=[VMEM] * 6,
        out_specs=(VMEM,) * 3,
        scratch_shapes=[
            pltpu.VMEM((blocks * windows, LANES), F32),
            pltpu.VMEM((classes * stations, freqs * LANES), F32),
        ],
        compiler_params=grant,
        cost_estimate=pl.CostEstimate(flops=flops, bytes_accessed=4 * 2**20, transcendentals=0),
    )(mine, other, pieces_of_green, onehot, own_table, weights)

    images = lax.all_to_all(image, ("freq", "sta"), 0, 0, tiled=True)
    new_slip = pl.pallas_call(
        update_kernel,
        out_shape=shape(slip.shape, F32),
        in_specs=[VMEM] * 4,
        out_specs=VMEM,
        compiler_params=grant,
    )(images, norm, slip, own)
    return new_slip, residual


def solution(mesh):
    n_freq = mesh.shape["freq"]
    placed = (
        P(None, ("grp", "freq", "tri")),
        P("freq", None, None, None),
        P("sta", None),
        P(None, ("grp", "freq"), "sta"),
        P(None, ("freq", "tri")),
        P("grp"),
    )

    def step(slip, green, pattern, observed, adjacency, smooth_weight):
        windows, block = slip.shape[0], green.shape[2]
        table = phase_table(green.shape[0] // n_freq * n_freq, windows, block)

        def body(*args):
            return local(*args, table=jnp.asarray(table))

        return jax.shard_map(
            body,
            mesh=mesh,
            in_specs=placed,
            out_specs=(P(None, ("grp", "freq", "tri")), P(None, ("grp", "freq"), "sta")),
            check_vma=False,
        )(slip, green, pattern, observed, adjacency, smooth_weight)

    return step
```

```python
import math

import jax
import jax.numpy as jnp
import numpy as np
from jax import lax
from jax.experimental import pallas as pl
from jax.experimental.pallas import tpu as pltpu
from jax.sharding import PartitionSpec as P

F32 = jnp.float32
BF16 = jnp.bfloat16
LANES = 128
CHUNK = 64


def phase_table(freq_total, windows, block):
    frequency = np.arange(freq_total, dtype=np.float32) + np.float32(1.0)
    window = np.arange(windows, dtype=np.float32) + np.float32(0.5)
    phases = np.float32(4.0 * math.pi / freq_total) * frequency[:, None] * window[None, :]
    phases = phases.astype(np.float64)
    both = np.stack([np.cos(phases), -np.sin(phases)], axis=-1).astype(np.float32)
    return np.repeat(both, block, axis=-1)


def split(value):
    high = value.astype(BF16)
    return high, (value - high.astype(F32)).astype(BF16)


def low_lanes(shape, block):
    return lax.broadcasted_iota(jnp.int32, shape, len(shape) - 1) < block


def spread_columns(read, parts, spread):
    def one(p, carry):
        value = read(p)
        for j in range(value.shape[1] // LANES):
            piece = value[:, j * LANES : (j + 1) * LANES]
            turned = pltpu.roll(piece, LANES // 2, 1)
            low = low_lanes(piece.shape, LANES // 2)
            row = (p * (value.shape[1] // LANES) + j) * 16
            row = row if isinstance(row, int) else pl.multiple_of(row, 16)
            spread[pl.ds(row, 8), :] = jnp.where(low, piece, turned)
            spread[pl.ds(row + 8, 8), :] = jnp.where(low, turned, piece)
        return carry

    if parts <= 8:
        for p in range(parts):
            one(p, 0)
    else:
        lax.fori_loop(0, parts, one, 0)


def onehot_of(doubled, classes):
    return jnp.concatenate([(doubled == k).astype(F32) for k in range(classes)], axis=0)


def over_chunks(count, step):
    if count == 1:
        step(0)
    else:
        lax.fori_loop(0, count, lambda n, carry: (step(n), carry)[1], 0)


def positions():
    freq = lax.axis_index("freq")
    return freq, freq * lax.axis_size("tri") + lax.axis_index("tri"), lax.axis_index("sta")


def ahead_kernel(out):
    out[...] = jnp.zeros(out.shape, F32)


def pack_kernel(slip, adjacency, out):
    windows, columns = slip.shape
    neighbours, triangles = adjacency.shape
    out[:, :columns] = slip[...]
    out[:neighbours, columns:] = adjacency[...].astype(F32)
    out[neighbours:, columns:] = jnp.zeros((windows - neighbours, triangles), F32)


def prepare_kernel(
    green_ref,
    pattern_ref,
    observed,
    table,
    ahead,
    green_out,
    onehot_out,
    turned_out,
    apart,
    table_out,
    ahead_out,
):
    freqs, classes, block, _ = green_ref.shape
    chunks, stations, _ = pattern_ref.shape
    first = positions()[0] * freqs
    ahead_out[...] = ahead[...]
    for f in range(freqs):
        for k in range(classes):
            high, low = split(green_ref[f, k])
            green_out[f, :block, k * LANES : (k + 1) * LANES] = high
            green_out[f, block:, k * LANES : (k + 1) * LANES] = low
        table_out[f] = table[first + f]

    def step(n):
        value = pattern_ref[n]
        onehot = onehot_of(jnp.concatenate([value, value], axis=1), classes)
        onehot_out[n] = onehot.astype(BF16)
        turned = onehot[:, :block].T.astype(BF16)
        turned_out[n] = jnp.concatenate([turned, turned], axis=1)

    over_chunks(chunks, step)
    for r in range(2):
        for j in range(stations // 2):
            piece = observed[r, :, j * LANES : (j + 1) * LANES]
            apart[r, 2 * j * freqs : (2 * j + 1) * freqs, :] = piece
            apart[r, (2 * j + 1) * freqs : (2 * j + 2) * freqs, :] = pltpu.roll(piece, block, 1)


def pattern_sums(spread, table, onehot_ref, summed):
    freqs, windows, _ = table.shape
    chunks = onehot_ref.shape[0]

    def step(n):
        base = n * CHUNK * windows
        fields = [spread[pl.ds(base + w, CHUNK, stride=windows), :] for w in range(windows)]
        spectra = []
        for f in range(freqs):
            total = table[f, 0:1] * fields[0]
            for w in range(1, windows):
                total = total + table[f, w : w + 1] * fields[w]
            spectra.append(jnp.concatenate(split(total), axis=0))
        product = jnp.dot(
            onehot_ref[n], jnp.concatenate(spectra, axis=1), preferred_element_type=F32
        )
        if chunks == 1:
            summed[...] = product
        else:
            summed[...] += product

    if chunks > 1:
        summed[...] = jnp.zeros_like(summed)
    over_chunks(chunks, step)


def predict_one(summed, green, f, stations, block):
    value = summed[:, f * LANES : (f + 1) * LANES]
    sign = jnp.where(low_lanes(value.shape, block), 1.0, -1.0)
    real = value * sign
    imag = pltpu.roll(value, block, 1)
    classes = value.shape[0] // stations
    rows = []
    for half in zip(split(real), split(imag)):
        for part in half:
            rows.append(
                jnp.concatenate(
                    [part[k * stations : (k + 1) * stations] for k in range(classes)], axis=1
                )
            )
    left = jnp.concatenate(rows, axis=0)
    out = lax.dot_general(left, green, (((1,), (1,)), ((), ())), preferred_element_type=F32)
    high = out[: 2 * stations]
    low = out[2 * stations :]
    total = high + jnp.where(low_lanes(low.shape, block), low, 0.0)
    return total + pltpu.roll(total, block, 1)


def forward_kernel(windows, codes, *refs):
    _, me, half = positions()
    count = max(len(codes), 1)
    pieces, refs = refs[:count], refs[count:]
    green, onehot_ref, turned_ref, apart, table, ahead, weight = refs[:7]
    missed, partial_out, weight_out = refs[7:10]
    weight_out[...] = ahead[...] + weight[...]
    if codes:
        shards, refs = refs[10], refs[11:]
        for (even, odd), piece in zip(codes, pieces):
            code = jnp.where(half == 0, even, odd).astype(jnp.int32)
            shards[lax.bitwise_xor(me, code)] = piece[:, : shards.shape[2]]
    else:
        shards, refs = pieces[0], refs[10:]
    spread, summed, adjoint_rows, fields = refs
    freqs, rows, _ = green.shape
    block = rows // 2
    stations = apart.shape[1] // freqs
    classes = summed.shape[0] // stations
    parts = shards.shape[0]
    width = partial_out.shape[3]
    low8 = low_lanes((freqs, LANES), block)
    spread_columns(lambda p: shards[p], parts, spread)
    pattern_sums(spread, table, onehot_ref, summed)
    predicted = [predict_one(summed, green[f], f, stations, block) for f in range(freqs)]
    lefts = []
    for f in range(freqs):
        seen = jnp.concatenate(
            [apart[r, pl.ds(f, stations, stride=freqs), :] for r in range(2)], axis=0
        )
        misfit = predicted[f] - seen
        for r in range(2):
            missed[r, pl.ds(f, stations, stride=freqs), :] = misfit[r * stations : (r + 1) * stations]
        low = low_lanes(misfit.shape, block)
        misfit = jnp.where(low, misfit, pltpu.roll(misfit, block, 1))
        high, rest = split(misfit)
        lefts.append(jnp.concatenate([high, rest[:, :block]], axis=1))
    sign = jnp.where(low_lanes((stations, LANES), block), 1.0, -1.0)
    for f in range(freqs):
        right = jnp.concatenate([green[f], green[f, :block]], axis=0)
        out = jnp.dot(lefts[f], right, preferred_element_type=F32)
        at = slice(f * LANES, (f + 1) * LANES)
        for k in range(classes):
            real = out[:stations, k * LANES : (k + 1) * LANES]
            imag = out[stations:, k * LANES : (k + 1) * LANES]
            high, rest = split(real * sign + pltpu.roll(imag, block, 1))
            adjoint_rows[k * stations : (k + 1) * stations, at] = high
            adjoint_rows[(classes + k) * stations : (classes + k + 1) * stations, at] = rest
    per_part = width // block
    chunk_parts = CHUNK // per_part

    def step(n):
        adjoint = jnp.dot(turned_ref[n], adjoint_rows[...], preferred_element_type=F32)
        for w in range(windows):
            total = table[0, w : w + 1, :] * adjoint[:, :LANES]
            for f in range(1, freqs):
                total = total + table[f, w : w + 1, :] * adjoint[:, f * LANES : (f + 1) * LANES]
            fields[pl.ds(w, CHUNK, stride=windows), :] = total + pltpu.roll(total, block, 1)
        for q in range(chunk_parts):
            p = n * chunk_parts + q
            side = lax.rem(p // (parts // 2) + half, 2)
            slot = lax.rem(jnp.asarray(p, jnp.int32), parts // 2)
            for j in range(per_part // 2):
                row = (q * per_part + 2 * j) * windows
                partial_out[side, slot, :, j * LANES : (j + 1) * LANES] = jnp.where(
                    low8, fields[row : row + windows, :], fields[row + windows : row + 2 * windows, :]
                )

    over_chunks(turned_ref.shape[0], step)


def residual_kernel(missed, residual_out):
    freqs = residual_out.shape[1]
    stations = missed.shape[1] // freqs
    block = residual_out.shape[2] // stations
    low8 = low_lanes((freqs, LANES), block)
    for r in range(2):
        for j in range(stations // 2):
            even = missed[r, 2 * j * freqs : (2 * j + 1) * freqs, :]
            odd = missed[r, (2 * j + 1) * freqs : (2 * j + 2) * freqs, :]
            residual_out[r, :, j * LANES : (j + 1) * LANES] = jnp.where(
                low8, even, pltpu.roll(odd, block, 1)
            )


def smooth_kernel(shards, weight, *refs):
    adjacency, out = refs[:-1], refs[-1]
    count, windows, width = out.shape
    parts = shards.shape[0]
    tris = len(adjacency)
    pieces = width // LANES
    lane = lax.broadcasted_iota(jnp.int32, (windows, LANES), 1)

    def pick(source, index):
        return jnp.take_along_axis(source, index, axis=1, mode="promise_in_bounds")

    out[...] = jnp.zeros(out.shape, F32)
    _, me, half = positions()
    for k in range(tris):
        p = me - lax.rem(me, tris) + lax.bitwise_xor(lax.rem(me, tris), jnp.int32(k))
        factor = jnp.where(p // count == half, weight[...], 0.0)
        around = [jnp.maximum(p - 1, 0), p, jnp.minimum(p + 1, parts - 1)]
        source = [shards[a, :, j * LANES : (j + 1) * LANES] for a in around for j in range(pieces)]
        for q in range(pieces):
            for j in range(3):
                start = width + (q // 2) * LANES
                row = adjacency[k][j : j + 1, start : start + LANES]
                row = jnp.broadcast_to(row, (windows, LANES))
                target = pick(row, (q % 2) * (LANES // 2) + lane // 2).astype(jnp.int32)
                if j == 0:
                    total = jnp.where(target < p * (width // 2), source[q], source[2 * pieces + q])
                    continue
                column = 2 * target + lane % 2 - (p - 1) * width
                inside = jnp.bitwise_and(column, LANES - 1)
                which = jnp.right_shift(column, 7)
                value = jnp.zeros((windows, LANES), F32)
                for v in range(q, q + 2 * pieces + 1):
                    value = jnp.where(which == v, pick(source[v], inside), value)
                total = total + value
            own = source[pieces + q]
            out[lax.rem(p, count), :, q * LANES : (q + 1) * LANES] = factor * (own - total / 3.0)


def image_kernel(
    mine, other, green, onehot_ref, table, weight, own_out, image_out, norm_out, spread, summed
):
    freqs, rows, _ = green.shape
    block = rows // 2
    classes = green.shape[2] // LANES
    stations = summed.shape[0] // classes
    count, windows, width = mine.shape
    _, me, half = positions()

    def read(p):
        slot = p % count if isinstance(p, int) else lax.rem(p, count)
        return jnp.where(p // count == half, mine[slot], other[slot])

    spread_columns(read, 2 * count, spread)
    pattern_sums(spread, table, onehot_ref, summed)
    slot = lax.rem(me, count)
    own_out[...] = jnp.where(me // count == half, mine[slot], other[slot])

    def squares(p, total):
        value = read(p)
        value = value * value
        for j in range(width // LANES):
            total = total + value[:, j * LANES : (j + 1) * LANES]
        return total

    numerator = jnp.zeros((windows, LANES), F32)
    if count <= 4:
        for p in range(2 * count):
            numerator = squares(p, numerator)
    else:
        numerator = lax.fori_loop(0, 2 * count, squares, numerator)
    image = jnp.zeros((8, LANES), F32)
    for f in range(freqs):
        predicted = predict_one(summed, green[f], f, stations, block)
        predicted = predicted * predicted
        for j in range(predicted.shape[0] // 8):
            image = image + predicted[8 * j : 8 * j + 8]
    image = jnp.where(low_lanes(image.shape, block), image, 0.0)
    image_out[...] = jnp.broadcast_to(jnp.sum(image), image_out.shape)
    norm_out[0] = jnp.broadcast_to(jnp.sum(numerator), norm_out.shape[1:])
    norm_out[1] = weight[...] * norm_out[0]


def update_kernel(images, norm, slip, own, out):
    image = images[0]
    for n in range(1, images.shape[0]):
        image = image + images[n]
    step = norm[0] / (image + norm[1])
    for j in range(slip.shape[1] // LANES):
        at = slice(j * LANES, (j + 1) * LANES)
        out[:, at] = jnp.maximum(slip[:, at] - step * own[:, at], 0.0)


VMEM = pl.BlockSpec(memory_space=pltpu.VMEM)


def local(slip, green, pattern, observed, adjacency, smooth_weight, *, table):
    n_freq, n_tri, n_sta = (lax.axis_size(a) for a in ("freq", "tri", "sta"))
    parts = n_freq * n_tri
    count = parts // n_sta
    freqs, classes, block, _ = green.shape
    windows, columns = slip.shape
    stations, blocks = pattern.shape
    pattern = pattern.reshape(stations, blocks // CHUNK, CHUNK).transpose(1, 0, 2)
    chunks = blocks // CHUNK
    grant = pltpu.CompilerParams(vmem_limit_bytes=(16 if chunks == 1 else 48) * 2**20)
    cores = [(0, 1), (1, 0)]
    shape = jax.ShapeDtypeStruct

    def across(value):
        return [
            lax.ppermute(value, "freq", [(i, i ^ k) for i in range(n_freq)])
            for k in range(1, n_freq)
        ]

    ahead = pl.pallas_call(
        ahead_kernel,
        out_shape=shape((8, LANES), F32),
        out_specs=VMEM,
        compiler_params=grant,
        cost_estimate=pl.CostEstimate(flops=10**10, bytes_accessed=2**10, transcendentals=0),
    )()
    adjacency, ahead = lax.optimization_barrier((adjacency, ahead))
    prepared = pl.pallas_call(
        prepare_kernel,
        out_shape=(
            shape((freqs, 2 * block, classes * 2 * block), BF16),
            shape((chunks, classes * stations, 2 * CHUNK), BF16),
            shape((chunks, CHUNK, 2 * classes * stations), BF16),
            shape((2, stations * freqs, LANES), F32),
            shape((freqs, windows, LANES), F32),
            shape((8, LANES), F32),
        ),
        in_specs=[VMEM] * 5,
        out_specs=(VMEM,) * 6,
        compiler_params=grant,
        cost_estimate=pl.CostEstimate(flops=10**6, bytes_accessed=6 * 2**20, transcendentals=0),
    )(green, pattern, observed, table, ahead)
    packed = pl.pallas_call(
        pack_kernel,
        out_shape=shape((windows, columns + adjacency.shape[1]), F32),
        in_specs=[VMEM] * 2,
        out_specs=VMEM,
        compiler_params=grant,
    )(slip, adjacency)
    neighbours = [packed] + [
        lax.ppermute(packed, "tri", [(i, i ^ k) for i in range(n_tri)]) for k in range(1, n_tri)
    ]
    if (n_freq, n_tri, n_sta) == (4, 2, 2):
        pieces = list(neighbours)
        codes = [(0, 0), (1, 1)]
        fetched = []
        order = range(n_freq - 1, 0, -1)
        for k in order:
            pairs = [
                (4 * (z ^ k) + 2 * (t ^ s) + s, 4 * z + 2 * t + s)
                for z in range(n_freq)
                for t in range(n_tri)
                for s in range(n_sta)
            ]
            fetched.append(lax.ppermute(slip, ("freq", "tri", "sta"), pairs))
            codes.append((2 * k, 2 * k + 1))
        fetched[0], prepared = lax.optimization_barrier((fetched[0], prepared))
        pieces += fetched + [lax.ppermute(v, "sta", cores) for v in fetched]
        codes += [(2 * k + 1, 2 * k) for k in order]
    else:
        copies = jnp.broadcast_to(slip[None], (parts,) + slip.shape)
        pieces = [lax.all_to_all(copies, ("freq", "tri"), 0, 0, tiled=True)]
        codes = []

    pieces_of_green, onehot, turned, apart, own_table, ahead = prepared
    flops = 2 * freqs * 128 * 1024 * 256
    whole = shape((parts,) + slip.shape, F32)
    outs = pl.pallas_call(
        lambda *refs: forward_kernel(windows, codes, *refs),
        out_shape=(
            shape((2, stations * freqs, LANES), F32),
            shape((n_sta, count, windows, columns), F32),
            shape((8, LANES), F32),
        )
        + ((whole,) if codes else ()),
        in_specs=[VMEM] * (len(pieces) + 7),
        out_specs=(VMEM,) * (4 if codes else 3),
        scratch_shapes=[
            pltpu.VMEM((blocks * windows, LANES), F32),
            pltpu.VMEM((classes * stations, freqs * LANES), F32),
            pltpu.VMEM((2 * classes * stations, freqs * LANES), BF16),
            pltpu.VMEM((CHUNK * windows, LANES), F32),
        ],
        compiler_params=grant,
        cost_estimate=pl.CostEstimate(flops=flops, bytes_accessed=4 * 2**20, transcendentals=0),
    )(*pieces, pieces_of_green, onehot, turned, apart, own_table, ahead, smooth_weight.reshape(1, 1))
    missed, partial, weights = outs[:3]
    shards = outs[3] if codes else pieces[0]

    residual = pl.pallas_call(
        residual_kernel,
        out_shape=shape(observed.shape, F32),
        in_specs=[VMEM],
        out_specs=VMEM,
        compiler_params=grant,
        cost_estimate=pl.CostEstimate(flops=10**6, bytes_accessed=2**20, transcendentals=0),
    )(missed)

    smooth = pl.pallas_call(
        smooth_kernel,
        out_shape=shape((count, windows, columns), F32),
        in_specs=[VMEM] * (2 + n_tri),
        out_specs=VMEM,
        compiler_params=grant,
        cost_estimate=pl.CostEstimate(flops=10**6, bytes_accessed=4 * 2**20, transcendentals=0),
    )(shards, weights, *neighbours)

    mine = partial[0] + lax.ppermute(partial[1], "sta", cores)
    mine = mine + smooth
    if n_freq <= 8:
        others = across(mine)
        others[-1], residual = lax.optimization_barrier((others[-1], residual))
        mine = sum(others, mine)
    else:
        mine = lax.psum(mine, "freq")
    other = lax.ppermute(mine, "sta", cores)

    ranks = n_freq * n_sta
    own, image, norm = pl.pallas_call(
        image_kernel,
        out_shape=(
            shape(slip.shape, F32),
            shape((ranks, 8, LANES), F32),
            shape((2, 8, LANES), F32),
        ),
        in_specs=[VMEM] * 6,
        out_specs=(VMEM,) * 3,
        scratch_shapes=[
            pltpu.VMEM((blocks * windows, LANES), F32),
            pltpu.VMEM((classes * stations, freqs * LANES), F32),
        ],
        compiler_params=grant,
        cost_estimate=pl.CostEstimate(flops=flops, bytes_accessed=4 * 2**20, transcendentals=0),
    )(mine, other, pieces_of_green, onehot, own_table, weights)

    images = lax.all_to_all(image, ("freq", "sta"), 0, 0, tiled=True)
    new_slip = pl.pallas_call(
        update_kernel,
        out_shape=shape(slip.shape, F32),
        in_specs=[VMEM] * 4,
        out_specs=VMEM,
        compiler_params=grant,
    )(images, norm, slip, own)
    return new_slip, residual


def solution(mesh):
    n_freq = mesh.shape["freq"]
    placed = (
        P(None, ("grp", "freq", "tri")),
        P("freq", None, None, None),
        P("sta", None),
        P(None, ("grp", "freq"), "sta"),
        P(None, ("freq", "tri")),
        P("grp"),
    )

    def step(slip, green, pattern, observed, adjacency, smooth_weight):
        windows, block = slip.shape[0], green.shape[2]
        table = phase_table(green.shape[0] // n_freq * n_freq, windows, block)

        def body(*args):
            return local(*args, table=jnp.asarray(table))

        return jax.shard_map(
            body,
            mesh=mesh,
            in_specs=placed,
            out_specs=(P(None, ("grp", "freq", "tri")), P(None, ("grp", "freq"), "sta")),
            check_vma=False,
        )(slip, green, pattern, observed, adjacency, smooth_weight)

    return step
```
